32 devices in a mesh: groups: 2 (over y), dp: 8 (over z, x), mp: 2 (over core).
Axes of the slice: x: 2, y: 2, z: 4, core: 2. Of those that a mesh axis runs over, the one named last changes fastest.
Arguments:
- acts: bfloat16 [2048, 4096], P(('groups', 'dp'), 'mp'), parts along dimension 0, may hold values from -45 to 45
- out_grads: bfloat16 [2048, 11008], P(('groups', 'dp'), 'mp'), parts along dimension 0, may hold values from -6 to 6
- in_proj: bfloat16 [4096, 32], P('mp'), may hold values from -0.09375 to 0.09375
- out_proj: bfloat16 [11008, 32], P('mp'), may hold values from -0.0546875 to 0.0546875
- example_ids: int32 [16, 128], P(('groups', 'dp')), parts along dimension 0, may hold values from 0 to 7, never falling along the last dimension, each value on 1 to 64 neighbouring positions
- query_ids: int32 [2048], P(('groups', 'mp')), parts along dimension 0, may hold values from 0 to 63
Outputs:
- scores: float32 [2048, 64], P(('groups', 'mp'), 'dp'), parts along dimension 0
The draws below stay inside these ranges and needn't reach their ends.
There are 2 independent parts, one for each index of `groups`. The reference program is written for one: setup_inputs(seed, part) draws one part's arguments, and reference() takes and returns one part's arrays. A program takes and returns all parts, laid end to end along the dimension named above; an argument that names none is the same for every part. Nothing has to cross between parts.
Inputs may be any that keep to these rules, and one draw needn't show every extreme that they name: `example_ids`: along each row the example numbers never fall; each of the 8 examples of a row has 1 to 64 tokens.
All inputs are finite; a program needn't handle non-finite values.
Results may differ from the reference program's by a relative error of at most 0.0003.
Values may be sent and summed in bfloat16 or wider, within the bound.
No kernel may reach another device: no remote copies, remote signals or barrier semaphores. Data moves between devices by JAX's collectives and lax.ppermute only.
A program may use at most 64 MiB of HBM per device.

```python
import math
import jax
import jax.numpy as jnp
import numpy as np
from jax import lax

D = 4096
FF = 11008
RIN = 32
ROUT = 32
TOK_DEV = 128
E_DEV = 8
QUERIES = 1024
K = 1024
TOKENS = 1024
EXAMPLES = 64
N_DP = 8


def draw_acts(key, part):
    key = jax.random.fold_in(key, 11)
    first, second = jax.random.split(key, 2)
    row = jnp.arange(TOKENS, dtype=jnp.float32)
    ramp = 1.0 + 2.0 * row / max(TOKENS - 1, 1)
    scale = jnp.exp(jax.random.uniform(second, (TOKENS,), minval=math.log(0.3), maxval=math.log(3.0)))
    base = jnp.clip(jax.random.normal(first, (TOKENS, D)), -5.0, 5.0)
    return (base * (ramp * scale)[:, None]).astype(jnp.bfloat16)


def touch_ends(array, stream_key, smallest, largest):
    longest = array.shape.index(max(array.shape))
    spots = []
    for shift in (0, 1):
        where = [jax.random.randint(jax.random.fold_in(stream_key, axis), (), 0, length) for axis, length in enumerate(array.shape)]
        where[longest] = (where[longest] + shift) % array.shape[longest]
        spots.append(tuple(where))
    return array.at[spots[0]].set(smallest).at[spots[1]].set(largest)


def block_scale(rng, shape, cuts, low, largest):
    def one(position, blocks):
        draws = jax.random.uniform(jax.random.fold_in(jax.random.fold_in(rng, 6), position), (blocks,), jnp.float32, low / len(cuts), largest / len(cuts))
        return jnp.repeat(jnp.exp(draws), shape[position] // blocks).reshape((-1,) + (1,) * (len(shape) - position - 1))

    gain = one(*cuts[0])
    for cut in cuts[1:]:
        gain = gain * one(*cut)
    return gain


def length_profile(number_of, total, reach, slope):
    portions = [(1 << 20) // math.isqrt(grade ** slope) + 1 for grade in range(2, number_of + 1)]
    rest, counts = total - reach - (number_of - 1), [1] * (number_of - 1)
    while rest > 0:
        candidates = [i for i in range(number_of - 1) if counts[i] < reach]
        pool, remaining = sum([portions[i] for i in candidates]), rest
        for i in candidates:
            addition = min(reach - counts[i], max(1, remaining * portions[i] // pool), rest)
            counts[i] = counts[i] + addition
            rest = rest - addition
    return np.array([reach] + counts)


def ragged(key, number_of, total, bound, slope):
    if number_of == 2:
        one = jax.random.randint(key, (), max(1, total - bound), min(bound, total - 1) + 1)
        return jnp.stack([one, total - one])
    tallies = jnp.asarray(length_profile(number_of, total, bound, slope), jnp.int32)
    twos = (number_of - 1) // 2
    source_of, receiver = tallies[1:1 + 2 * twos:2], tallies[2:2 + 2 * twos:2]
    margin = jnp.minimum(source_of - 1, bound - receiver)
    shifted = jax.random.randint(jax.random.fold_in(key, 1), (twos,), 0, 1 << 20) % (margin + 1)
    tallies = tallies.at[1:1 + 2 * twos:2].set(source_of - shifted).at[2:2 + 2 * twos:2].set(receiver + shifted)
    return tallies[jax.random.permutation(jax.random.fold_in(key, 2), number_of)]


def gaussian(own_key, extent, deviation, limit, pieces=(), kind=jnp.bfloat16):
    entries = deviation * jax.random.normal(own_key, extent, jnp.float32)
    if pieces:
        entries = entries * block_scale(own_key, extent, pieces, -0.22, 0.18)
    return jnp.clip(entries, -limit, limit).astype(kind)


def setup_inputs(seed: int = 0, part: int = 0) -> dict:
    arg_keys = jax.random.split(jax.random.key(seed), 7)
    part_splits = jax.random.split(jax.random.fold_in(arg_keys[6], part), 7)
    return {
        "acts": draw_acts(jax.random.fold_in(jax.random.fold_in(arg_keys[6], part), 71), part),
        "out_grads": gaussian(part_splits[1], (TOKENS, FF), 1.0, 6.0, ((0, 8), (1, 2))),
        "in_proj": gaussian(arg_keys[2], (D, RIN), D ** -0.5, 0.09375, ((0, 2),)),
        "out_proj": gaussian(arg_keys[3], (FF, ROUT), FF ** -0.5, 0.0546875, ((0, 2),)),
        "example_ids": jax.vmap(lambda own: jnp.searchsorted(jnp.cumsum(ragged(own, E_DEV, TOK_DEV, TOK_DEV // 2, 1)), jnp.arange(TOK_DEV), side="right"))(jax.random.split(part_splits[4], N_DP)).reshape((N_DP, TOK_DEV)).astype(jnp.int32),
        "query_ids": touch_ends(jax.random.randint(part_splits[5], (QUERIES,), 0, EXAMPLES), jax.random.fold_in(part_splits[5], 1), 0, EXAMPLES - 1).astype(jnp.int32),
    }


def chol_solve(factor, rhs):
    inner = lax.linalg.triangular_solve(factor, rhs, left_side=True, lower=True)
    return lax.linalg.triangular_solve(factor, inner, left_side=True, lower=True, transpose_a=True)

def reference(acts, out_grads, in_proj, out_proj, example_ids, query_ids):
    proj_in = jnp.dot(acts.astype(jnp.float32), in_proj.astype(jnp.float32), preferred_element_type=jnp.float32).astype(jnp.bfloat16)
    proj_out = jnp.dot(out_grads.astype(jnp.float32), out_proj.astype(jnp.float32), preferred_element_type=jnp.float32).astype(jnp.bfloat16)
    shard_in = proj_in.reshape(N_DP, TOK_DEV, RIN)
    shard_out = proj_out.reshape(N_DP, TOK_DEV, ROUT)

    def one_shard(items):
        left, right, ids = items
        onehot = (ids[:, None] == jnp.arange(E_DEV, dtype=jnp.int32)[None, :]).astype(jnp.float32)
        wide = (onehot[:, :, None] * left.astype(jnp.float32)[:, None, :]).reshape(TOK_DEV, E_DEV * RIN)
        summed = lax.dot_general(right.astype(jnp.float32), wide, (((0,), (0,)), ((), ())), precision=lax.Precision.HIGHEST)
        return summed.reshape(ROUT, E_DEV, RIN).transpose(1, 0, 2).reshape(E_DEV, K)
    sketches = lax.map(one_shard, (shard_in, shard_out, example_ids))
    sketches = sketches.reshape(EXAMPLES, K).astype(jnp.bfloat16)
    gram = lax.dot_general(sketches.astype(jnp.float32), sketches.astype(jnp.float32), (((0,), (0,)), ((), ())), preferred_element_type=jnp.float32)
    wide_sk = sketches.astype(jnp.float32)
    damping = 0.1 * jnp.sum(wide_sk * wide_sk) / K
    damped = gram + damping * jnp.eye(K, dtype=jnp.float32)
    factor = jnp.linalg.cholesky(damped)
    queried = jnp.take(wide_sk, query_ids, axis=0)
    precond = chol_solve(factor, queried.T)
    return lax.dot_general(precond, wide_sk, (((0,), (1,)), ((), ())), precision=lax.Precision.HIGHEST)
```

```python
import jax
import jax.numpy as jnp
from jax import lax
from jax.experimental import pallas as pl
from jax.experimental.pallas import tpu as pltpu
from jax.sharding import PartitionSpec as P

E_DEV = 8
LANES = 128
NT = (((1,), (1,)), ((), ()))
STEPS = ((4, 4), (3, 7), (1, 5), (2, 6))


def chunks(size, parts):
    per = -(-size // (parts * LANES)) * LANES
    starts = range(0, size, per)
    return [(s, min(per, size - s)) for s in starts]


def project(acts, out_grads, in_t, out_t):
    rin, rout = in_t.shape[0], out_t.shape[0]
    tok = acts.shape[0]
    a_cuts, g_cuts = chunks(acts.shape[1], 2), chunks(out_grads.shape[1], 4)

    def kernel(a_hbm, g_hbm, i_hbm, o_hbm, out_ref, a_v, g_v, i_v, o_v, sems):
        copies = []

        def start(src, dst):
            copy = pltpu.make_async_copy(src, dst, sems.at[len(copies)])
            copy.start()
            copies.append(copy)
            return copy

        i_copy = start(i_hbm, i_v)
        a_copies = [start(a_hbm.at[:, pl.ds(s, n)], a_v.at[:, pl.ds(s, n)]) for s, n in a_cuts]
        o_copy = start(o_hbm, o_v)
        g_copies = [start(g_hbm.at[:, pl.ds(s, n)], g_v.at[:, pl.ds(s, n)]) for s, n in g_cuts]

        def side(w_copy, w_v, x_copies, x_v, cuts):
            w_copy.wait()
            total = None
            for copy, (s, n) in zip(x_copies, cuts):
                copy.wait()
                term = lax.dot_general(
                    w_v[:, s : s + n], x_v[:, s : s + n], NT, preferred_element_type=jnp.float32
                )
                total = term if total is None else total + term
            return total

        out_ref[0:rin, :] = side(i_copy, i_v, a_copies, a_v, a_cuts)
        out_ref[rin : rin + rout, :] = side(o_copy, o_v, g_copies, g_v, g_cuts)

    hbm = pl.BlockSpec(memory_space=pl.ANY)
    return pl.pallas_call(
        kernel,
        out_shape=jax.ShapeDtypeStruct((rin + rout, tok), jnp.float32),
        in_specs=[hbm] * 4,
        out_specs=pl.BlockSpec(memory_space=pltpu.VMEM),
        scratch_shapes=[
            pltpu.VMEM(acts.shape, acts.dtype),
            pltpu.VMEM(out_grads.shape, out_grads.dtype),
            pltpu.VMEM(in_t.shape, in_t.dtype),
            pltpu.VMEM(out_t.shape, out_t.dtype),
            pltpu.SemaphoreType.DMA((2 + len(a_cuts) + len(g_cuts),)),
        ],
        compiler_params=pltpu.CompilerParams(vmem_limit_bytes=16 * 2**20),
        name="project",
    )(acts, out_grads, in_t, out_t)


def sketch(mine, other, ids, rin):
    rout = mine.shape[0] - rin
    tok = mine.shape[1]
    groups = LANES // rin
    o_per = rout // groups

    def kernel(mine_ref, other_ref, ids_ref, out_ref):
        both = (mine_ref[...] + other_ref[...]).astype(jnp.bfloat16)
        left = both[0:rin]
        right = both[rin : rin + rout].astype(jnp.float32)
        member = lax.broadcasted_iota(jnp.int32, (E_DEV, tok), 0) == ids_ref[...]
        member = jnp.where(member, 1.0, 0.0)
        zero = jnp.zeros((rin, tok), jnp.bfloat16)
        columns, rows = [], []
        for g in range(groups):
            masked = [member * right[g * o_per + o : g * o_per + o + 1] for o in range(o_per)]
            columns.append(jnp.concatenate(masked, axis=0).astype(jnp.bfloat16))
            rows.append(jnp.concatenate([left if h == g else zero for h in range(groups)], axis=1))
        out_ref[...] = lax.dot_general(
            jnp.concatenate(columns, axis=1),
            jnp.concatenate(rows, axis=0),
            NT,
            preferred_element_type=jnp.float32,
        ).astype(jnp.bfloat16)

    return pl.pallas_call(
        kernel,
        out_shape=jax.ShapeDtypeStruct((o_per * E_DEV, LANES), jnp.bfloat16),
        name="sketch",
    )(mine, other, ids)


def solve(blocks, owners, query_ids):
    count = len(blocks)
    size = count * E_DEV
    k_size = blocks[0].shape[0] * LANES // E_DEV
    queries = query_ids.shape[1]

    def kernel(*refs):
        block_refs, owner_ref, ids_ref, out_ref = refs[:count], refs[count], refs[count + 1], refs[count + 2]

        def flat(ref):
            block = ref[...].astype(jnp.float32)
            cuts = [block[r : r + E_DEV] for r in range(0, block.shape[0], E_DEV)]
            return jnp.concatenate(cuts, axis=1)

        every = jnp.concatenate([flat(ref) for ref in block_refs], axis=0).astype(jnp.bfloat16)
        twice = jnp.concatenate([every, every], axis=0)
        gram = lax.dot_general(every, twice, NT, preferred_element_type=jnp.float32)
        row = lax.broadcasted_iota(jnp.int32, (size, 2 * size), 0)
        lane = lax.broadcasted_iota(jnp.int32, (size, 2 * size), 1)
        diagonal = row == lane
        damping = 0.1 * jnp.sum(jnp.where(diagonal, gram, 0.0)) / k_size
        right_eye = jnp.where(row + size == lane, 1.0, 0.0)
        system = jnp.where(lane < size, gram + jnp.where(diagonal, damping, 0.0), right_eye)
        table = [system[r : r + E_DEV] for r in range(0, size, E_DEV)]
        shape = table[0].shape
        sub = lax.broadcasted_iota(jnp.int32, shape, 0)

        def down(value, i):
            return jnp.broadcast_to(value[i : i + 1], shape)

        for k in range(count):
            wide = [[jnp.broadcast_to(t[:, c : c + 1], shape) for c in range(k * E_DEV, (k + 1) * E_DEV)] for t in table]
            pivot, cols = table[k], wide[k]
            for i in range(E_DEV):
                scale = 1.0 / down(cols[i], i)
                here = sub == i
                factor = cols[i]

                def clear(value):
                    line = down(value, i) * scale
                    return jnp.where(here, line, value - factor * line)

                pivot = clear(pivot)
                cols = [clear(c) if j > i else c for j, c in enumerate(cols)]
            table[k] = pivot
            lines = [down(pivot, j) for j in range(E_DEV)]
            for r in range(count):
                if r != k:
                    drop = wide[r][0] * lines[0]
                    for j in range(1, E_DEV):
                        drop = drop + wide[r][j] * lines[j]
                    table[r] = table[r] - drop
        eye = jnp.where(sub + size == lane[0:E_DEV], 1.0, 0.0)
        result = jnp.where(lane[0:E_DEV] >= size, eye - damping * table[0], 0.0)

        spot = lax.broadcasted_iota(jnp.int32, (2 * size, queries), 0)
        place = (spot - size) // E_DEV
        example = jnp.full_like(spot, -1)
        for b in range(count):
            example = jnp.where(place == b, owner_ref[b] * E_DEV, example)
        example = example + spot % E_DEV
        chosen = jnp.where((spot >= size) & (example == ids_ref[...]), 1.0, 0.0).astype(jnp.bfloat16)
        high = result.astype(jnp.bfloat16)
        rest = result - high.astype(jnp.float32)
        mid = rest.astype(jnp.bfloat16)
        low = (rest - mid.astype(jnp.float32)).astype(jnp.bfloat16)
        picks = [jnp.dot(part, chosen, preferred_element_type=jnp.float32) for part in (high, mid, low)]
        out_ref[...] = picks[0] + (picks[1] + picks[2])

    vmem = pl.BlockSpec(memory_space=pltpu.VMEM)
    return pl.pallas_call(
        kernel,
        out_shape=jax.ShapeDtypeStruct((E_DEV, queries), jnp.float32),
        in_specs=[vmem] * count + [pl.BlockSpec(memory_space=pltpu.SMEM), vmem],
        out_specs=vmem,
        name="solve",
    )(*blocks, owners, query_ids)


def fetch(value, pair, count):
    moves = [(2 * i + c, 2 * (i ^ pair[c]) + c) for i in range(count) for c in range(2)]
    return lax.ppermute(value, ("dp", "mp"), moves)


def swap(value):
    return lax.ppermute(value, "mp", [(0, 1), (1, 0)])


def local_small(acts, out_grads, in_proj, out_proj, example_ids, query_ids):
    count = lax.axis_size("dp")
    mine = project(acts, out_grads, in_proj.T, out_proj.T)
    own = sketch(mine, swap(mine), example_ids, in_proj.shape[1])
    near = [fetch(own, pair, count) for pair in STEPS]
    far = [swap(block) for block in near[1:]]
    core = lax.axis_index("mp")
    steps = jnp.array(
        [[0] + [p[c] for p in STEPS] + [p[1 - c] for p in STEPS[1:]] for c in range(2)], jnp.int32
    )
    owners = steps[core] ^ lax.axis_index("dp")
    picked = solve([own] + near + far, owners, query_ids.reshape(1, -1))
    return picked.T


def chol_solve(factor, rhs):
    inner = lax.linalg.triangular_solve(factor, rhs, left_side=True, lower=True)
    return lax.linalg.triangular_solve(factor, inner, left_side=True, lower=True, transpose_a=True)


def local_large(acts, out_grads, in_proj, out_proj, example_ids, query_ids):
    part_in = jnp.dot(acts, in_proj, preferred_element_type=jnp.float32)
    part_out = jnp.dot(out_grads, out_proj, preferred_element_type=jnp.float32)
    full_in, full_out = lax.psum((part_in, part_out), "mp")
    left = full_in.astype(jnp.bfloat16)
    right = full_out.astype(jnp.bfloat16)
    tok_count = left.shape[0]
    rin_size = left.shape[1]
    rout_size = right.shape[1]
    k_size = rin_size * rout_size
    ids = example_ids[0]
    onehot = (ids[:, None] == jnp.arange(E_DEV, dtype=jnp.int32)[None, :]).astype(jnp.bfloat16)
    wide = (onehot[:, :, None] * left[:, None, :]).reshape(tok_count, E_DEV * rin_size)
    summed = lax.dot_general(
        right, wide, (((0,), (0,)), ((), ())), preferred_element_type=jnp.float32
    )
    local_sk = (
        summed.reshape(rout_size, E_DEV, rin_size)
        .transpose(1, 0, 2)
        .reshape(E_DEV, k_size)
        .astype(jnp.bfloat16)
    )
    every_sk = lax.all_gather(local_sk, "dp", axis=0, tiled=True)
    gram = lax.dot_general(
        every_sk, every_sk, (((0,), (0,)), ((), ())), preferred_element_type=jnp.float32
    )
    local_f32 = local_sk.astype(jnp.float32)
    total_sq = lax.psum(jnp.sum(local_f32 * local_f32), "dp")
    damping = 0.1 * total_sq / k_size
    damped = gram + damping * jnp.eye(k_size, dtype=jnp.float32)
    factor = jnp.linalg.cholesky(damped)
    queried = jnp.take(every_sk, query_ids, axis=0).astype(jnp.float32)
    precond = chol_solve(factor, queried.T)
    return lax.dot_general(
        precond, local_f32, (((0,), (1,)), ((), ())), precision=lax.Precision.HIGHEST
    )


def solution(mesh):
    in_specs = (
        P(("groups", "dp"), "mp"),
        P(("groups", "dp"), "mp"),
        P("mp", None),
        P("mp", None),
        P(("groups", "dp"), None),
        P(("groups", "mp")),
    )
    out_specs = P(("groups", "mp"), "dp")
    small = mesh.shape["dp"] == 8 and mesh.shape["mp"] == 2
    local = local_small if small else local_large
    return jax.shard_map(local, mesh=mesh, in_specs=in_specs, out_specs=out_specs, check_vma=False)
```

```python
import jax
import jax.numpy as jnp
from jax import lax
from jax.experimental import pallas as pl
from jax.experimental.pallas import tpu as pltpu
from jax.sharding import PartitionSpec as P

E_DEV = 8
LANES = 128
NT = (((1,), (1,)), ((), ()))
STEPS = ((4, 4), (3, 7), (1, 5), (2, 6))
ORDER = ((0, 0),) + STEPS + tuple((b, a) for a, b in STEPS[1:])


def chunks(size, parts):
    per = -(-size // (parts * LANES)) * LANES
    starts = range(0, size, per)
    return [(s, min(per, size - s)) for s in starts]


def project(acts, out_grads, in_t, out_t, example_ids, query_ids):
    rin, rout = in_t.shape[0], out_t.shape[0]
    tok = acts.shape[0]
    g_cuts = chunks(out_grads.shape[1], 2)

    def kernel(a_hbm, g_hbm, i_hbm, o_hbm, e_hbm, q_hbm, out_ref, e_ref, q_ref, a_v, g_v, i_v, o_v, sems):
        copies = []

        def start(src, dst):
            copy = pltpu.make_async_copy(src, dst, sems.at[len(copies)])
            copy.start()
            copies.append(copy)
            return copy

        i_copy = start(i_hbm, i_v)
        a_copy = start(a_hbm, a_v)
        o_copy = start(o_hbm, o_v)
        g_copies = [start(g_hbm.at[:, pl.ds(s, n)], g_v.at[:, pl.ds(s, n)]) for s, n in g_cuts]
        e_copy = start(e_hbm, e_ref)
        q_copy = start(q_hbm, q_ref)
        i_copy.wait()
        a_copy.wait()
        out_ref[0:rin, :] = lax.dot_general(i_v[...], a_v[...], NT, preferred_element_type=jnp.float32)
        o_copy.wait()
        total = None
        for copy, (s, n) in zip(g_copies, g_cuts):
            copy.wait()
            term = lax.dot_general(o_v[:, s : s + n], g_v[:, s : s + n], NT, preferred_element_type=jnp.float32)
            total = term if total is None else total + term
        out_ref[rin : rin + rout, :] = total
        e_copy.wait()
        q_copy.wait()

    hbm = pl.BlockSpec(memory_space=pltpu.HBM)
    vmem = pl.BlockSpec(memory_space=pltpu.VMEM)
    operands = (acts, out_grads, in_t, out_t, example_ids, query_ids)
    return pl.pallas_call(
        kernel,
        out_shape=[
            jax.ShapeDtypeStruct((rin + rout, tok), jnp.float32),
            jax.ShapeDtypeStruct(example_ids.shape, example_ids.dtype),
            jax.ShapeDtypeStruct(query_ids.shape, query_ids.dtype),
        ],
        in_specs=[hbm] * 6,
        out_specs=[vmem] * 3,
        scratch_shapes=[
            pltpu.VMEM(acts.shape, acts.dtype),
            pltpu.VMEM(out_grads.shape, out_grads.dtype),
            pltpu.VMEM(in_t.shape, in_t.dtype),
            pltpu.VMEM(out_t.shape, out_t.dtype),
            pltpu.SemaphoreType.DMA((5 + len(g_cuts),)),
        ],
        compiler_params=pltpu.CompilerParams(vmem_limit_bytes=16 * 2**20),
        name="project",
    )(*[pltpu.with_memory_space_constraint(x, pltpu.HBM) for x in operands])


def sketch(mine, other, ids, rin):
    rout = mine.shape[0] - rin
    tok = mine.shape[1]
    groups = LANES // rin
    o_per = rout // groups

    def kernel(mine_ref, other_ref, ids_ref, out_ref):
        both = (mine_ref[...] + other_ref[...]).astype(jnp.bfloat16)
        left = both[0:rin]
        right = both[rin : rin + rout].astype(jnp.float32)
        member = lax.broadcasted_iota(jnp.int32, (E_DEV, tok), 0) == ids_ref[...]
        member = jnp.where(member, 1.0, 0.0)
        zero = jnp.zeros((rin, tok), jnp.bfloat16)
        columns, rows = [], []
        for g in range(groups):
            masked = [member * right[g * o_per + o : g * o_per + o + 1] for o in range(o_per)]
            columns.append(jnp.concatenate(masked, axis=0).astype(jnp.bfloat16))
            rows.append(jnp.concatenate([left if h == g else zero for h in range(groups)], axis=1))
        out_ref[...] = lax.dot_general(
            jnp.concatenate(columns, axis=1),
            jnp.concatenate(rows, axis=0),
            NT,
            preferred_element_type=jnp.float32,
        ).astype(jnp.bfloat16)

    return pl.pallas_call(
        kernel,
        out_shape=jax.ShapeDtypeStruct((o_per * E_DEV, LANES), jnp.bfloat16),
        compiler_params=pltpu.CompilerParams(vmem_limit_bytes=4 * 2**20),
        name="sketch",
    )(mine, other, ids)


def solve(blocks, query_ids):
    count = len(blocks)
    size = count * E_DEV
    k_size = blocks[0].shape[0] * LANES // E_DEV
    queries = query_ids.shape[1]

    def kernel(*refs):
        block_refs, ids_ref, out_ref = refs[:count], refs[count], refs[count + 1]

        def flat(ref):
            block = ref[...].astype(jnp.float32)
            cuts = [block[r : r + E_DEV] for r in range(0, block.shape[0], E_DEV)]
            return jnp.concatenate(cuts, axis=1)

        every = jnp.concatenate([flat(ref) for ref in block_refs], axis=0).astype(jnp.bfloat16)
        twice = jnp.concatenate([every, every], axis=0)
        gram = lax.dot_general(every, twice, NT, preferred_element_type=jnp.float32)
        row = lax.broadcasted_iota(jnp.int32, (size, 2 * size), 0)
        lane = lax.broadcasted_iota(jnp.int32, (size, 2 * size), 1)
        diagonal = row == lane
        damping = 0.1 * jnp.sum(jnp.where(diagonal, gram, 0.0)) / k_size
        right_eye = jnp.where(row + size == lane, 1.0, 0.0)
        system = jnp.where(lane < size, gram + jnp.where(diagonal, damping, 0.0), right_eye)
        table = [system[r : r + E_DEV] for r in range(0, size, E_DEV)]
        shape = table[0].shape
        sub = lax.broadcasted_iota(jnp.int32, shape, 0)

        def down(value, i):
            return jnp.broadcast_to(value[i : i + 1], shape)

        for k in range(count):
            wide = [[jnp.broadcast_to(t[:, c : c + 1], shape) for c in range(k * E_DEV, (k + 1) * E_DEV)] for t in table]
            pivot, cols = table[k], wide[k]
            for i in range(E_DEV):
                scale = 1.0 / down(cols[i], i)
                here = sub == i
                factor = cols[i]

                def clear(value):
                    line = down(value, i) * scale
                    return jnp.where(here, line, value - factor * line)

                pivot = clear(pivot)
                cols = [clear(c) if j > i else c for j, c in enumerate(cols)]
            table[k] = pivot
            lines = [down(pivot, j) for j in range(E_DEV)]
            for r in range(count):
                if r != k:
                    drop = wide[r][0] * lines[0]
                    for j in range(1, E_DEV):
                        drop = drop + wide[r][j] * lines[j]
                    table[r] = table[r] - drop
        eye = jnp.where(sub + size == lane[0:E_DEV], 1.0, 0.0)
        result = jnp.where(lane[0:E_DEV] >= size, eye - damping * table[0], 0.0)

        spot = lax.broadcasted_iota(jnp.int32, (2 * size, queries), 0)
        place = (spot - size) // E_DEV
        here, core = lax.axis_index("dp"), lax.axis_index("mp")
        example = jnp.full_like(spot, -1)
        for b, pair in enumerate(ORDER):
            owner = here ^ jnp.where(core == 0, pair[0], pair[1])
            example = jnp.where(place == b, owner * E_DEV, example)
        example = example + spot % E_DEV
        chosen = jnp.where((spot >= size) & (example == ids_ref[...]), 1.0, 0.0).astype(jnp.bfloat16)
        high = result.astype(jnp.bfloat16)
        rest = result - high.astype(jnp.float32)
        mid = rest.astype(jnp.bfloat16)
        low = (rest - mid.astype(jnp.float32)).astype(jnp.bfloat16)
        picks = [jnp.dot(part, chosen, preferred_element_type=jnp.float32) for part in (high, mid, low)]
        out_ref[...] = picks[0] + (picks[1] + picks[2])

    vmem = pl.BlockSpec(memory_space=pltpu.VMEM)
    return pl.pallas_call(
        kernel,
        out_shape=jax.ShapeDtypeStruct((E_DEV, queries), jnp.float32),
        in_specs=[vmem] * (count + 1),
        out_specs=vmem,
        compiler_params=pltpu.CompilerParams(vmem_limit_bytes=8 * 2**20),
        name="solve",
    )(*blocks, query_ids)


def fetch(value, pair, count):
    moves = [(2 * i + c, 2 * (i ^ pair[c]) + c) for i in range(count) for c in range(2)]
    return lax.ppermute(value, ("dp", "mp"), moves)


def swap(value):
    return lax.ppermute(value, "mp", [(0, 1), (1, 0)])


def local_small(acts, out_grads, in_proj, out_proj, example_ids, query_ids):
    count = lax.axis_size("dp")
    mine, ids, queries = project(
        acts, out_grads, in_proj.T, out_proj.T, example_ids, query_ids.reshape(1, -1)
    )
    own = sketch(mine, swap(mine), ids, in_proj.shape[1])
    near = [fetch(own, pair, count) for pair in STEPS]
    far = [swap(block) for block in near[1:]]
    return solve([own] + near + far, queries).T


def chol_solve(factor, rhs):
    inner = lax.linalg.triangular_solve(factor, rhs, left_side=True, lower=True)
    return lax.linalg.triangular_solve(factor, inner, left_side=True, lower=True, transpose_a=True)


def local_large(acts, out_grads, in_proj, out_proj, example_ids, query_ids):
    part_in = jnp.dot(acts, in_proj, preferred_element_type=jnp.float32)
    part_out = jnp.dot(out_grads, out_proj, preferred_element_type=jnp.float32)
    full_in, full_out = lax.psum((part_in, part_out), "mp")
    left = full_in.astype(jnp.bfloat16)
    right = full_out.astype(jnp.bfloat16)
    tok_count = left.shape[0]
    rin_size = left.shape[1]
    rout_size = right.shape[1]
    k_size = rin_size * rout_size
    ids = example_ids[0]
    onehot = (ids[:, None] == jnp.arange(E_DEV, dtype=jnp.int32)[None, :]).astype(jnp.bfloat16)
    wide = (onehot[:, :, None] * left[:, None, :]).reshape(tok_count, E_DEV * rin_size)
    summed = lax.dot_general(
        right, wide, (((0,), (0,)), ((), ())), preferred_element_type=jnp.float32
    )
    local_sk = (
        summed.reshape(rout_size, E_DEV, rin_size)
        .transpose(1, 0, 2)
        .reshape(E_DEV, k_size)
        .astype(jnp.bfloat16)
    )
    every_sk = lax.all_gather(local_sk, "dp", axis=0, tiled=True)
    gram = lax.dot_general(
        every_sk, every_sk, (((0,), (0,)), ((), ())), preferred_element_type=jnp.float32
    )
    local_f32 = local_sk.astype(jnp.float32)
    total_sq = lax.psum(jnp.sum(local_f32 * local_f32), "dp")
    damping = 0.1 * total_sq / k_size
    damped = gram + damping * jnp.eye(k_size, dtype=jnp.float32)
    factor = jnp.linalg.cholesky(damped)
    queried = jnp.take(every_sk, query_ids, axis=0).astype(jnp.float32)
    precond = chol_solve(factor, queried.T)
    return lax.dot_general(
        precond, local_f32, (((0,), (1,)), ((), ())), precision=lax.Precision.HIGHEST
    )


def solution(mesh):
    in_specs = (
        P(("groups", "dp"), "mp"),
        P(("groups", "dp"), "mp"),
        P("mp", None),
        P("mp", None),
        P(("groups", "dp"), None),
        P(("groups", "mp")),
    )
    out_specs = P(("groups", "mp"), "dp")
    small = mesh.shape["dp"] == 8 and mesh.shape["mp"] == 2
    local = local_small if small else local_large
    return jax.shard_map(local, mesh=mesh, in_specs=in_specs, out_specs=out_specs, check_vma=False)
```

```python
import jax
import jax.numpy as jnp
from jax import lax
from jax.experimental import pallas as pl
from jax.experimental.pallas import tpu as pltpu
from jax.sharding import PartitionSpec as P

E_DEV = 8
LANES = 128
NT = (((1,), (1,)), ((), ()))
STEPS = (
    ((5, 7, 0, 6, 2, 3, 4, 1), (5, 7, 0, 6, 2, 3, 4, 1)),
    ((4, 0, 5, 1, 6, 2, 7, 3), (7, 5, 6, 0, 1, 4, 3, 2)),
    ((2, 6, 3, 7, 0, 1, 5, 4), (6, 2, 7, 4, 3, 0, 1, 5)),
    ((1, 3, 4, 2, 5, 7, 0, 6), (3, 4, 1, 5, 7, 6, 2, 0)),
)


def places(chip, core):
    blocks = [chip]
    blocks += [step[core].index(chip) for step in STEPS]
    blocks += [step[1 - core].index(chip) for step in STEPS[1:]]
    return sum(blocks.index(owner) << (4 * owner) for owner in range(len(blocks)))


def chunks(size, parts):
    per = -(-size // (parts * LANES)) * LANES
    starts = range(0, size, per)
    return [(s, min(per, size - s)) for s in starts]


def project(acts, out_grads, in_t, out_t, example_ids, query_ids, count):
    rin, rout = in_t.shape[0], out_t.shape[0]
    tok = acts.shape[0]
    queries = query_ids.shape[1]
    g_cuts = chunks(out_grads.shape[1], 2)

    def kernel(a_hbm, g_hbm, i_hbm, o_hbm, e_hbm, q_hbm, out_ref, e_ref, pick_ref, a_v, g_v, i_v, o_v, q_v, sems):
        copies = []

        def start(src, dst):
            copy = pltpu.make_async_copy(src, dst, sems.at[len(copies)])
            copy.start()
            copies.append(copy)
            return copy

        q_copy = start(q_hbm, q_v)
        i_copy = start(i_hbm, i_v)
        a_copy = start(a_hbm, a_v)
        o_copy = start(o_hbm, o_v)
        g_copies = [start(g_hbm.at[:, pl.ds(s, n)], g_v.at[:, pl.ds(s, n)]) for s, n in g_cuts]
        e_copy = start(e_hbm, e_ref)
        q_copy.wait()
        device = lax.axis_index("dp") * 2 + lax.axis_index("mp")
        code = jnp.int32(0)
        for n in range(2 * count):
            bits = places(n // 2, n % 2)
            code = jnp.where(device == n, bits - (bits >> 31 << 32), code)
        ids = q_v[...]
        spot = ((code >> (ids // E_DEV * 4)) & 7) * E_DEV + ids % E_DEV
        row = lax.broadcasted_iota(jnp.int32, pick_ref.shape, 0)
        pick_ref[...] = jnp.where(row == spot, 1.0, 0.0).astype(jnp.bfloat16)
        i_copy.wait()
        a_copy.wait()
        out_ref[0:rin, :] = lax.dot_general(i_v[...], a_v[...], NT, preferred_element_type=jnp.float32)
        o_copy.wait()
        total = None
        for copy, (s, n) in zip(g_copies, g_cuts):
            copy.wait()
            term = lax.dot_general(o_v[:, s : s + n], g_v[:, s : s + n], NT, preferred_element_type=jnp.float32)
            total = term if total is None else total + term
        out_ref[rin : rin + rout, :] = total
        e_copy.wait()

    hbm = pl.BlockSpec(memory_space=pltpu.HBM)
    vmem = pl.BlockSpec(memory_space=pltpu.VMEM)
    operands = (acts, out_grads, in_t, out_t, example_ids, query_ids)
    return pl.pallas_call(
        kernel,
        out_shape=[
            jax.ShapeDtypeStruct((rin + rout, tok), jnp.float32),
            jax.ShapeDtypeStruct(example_ids.shape, example_ids.dtype),
            jax.ShapeDtypeStruct((count * E_DEV, queries), jnp.bfloat16),
        ],
        in_specs=[hbm] * 6,
        out_specs=[vmem] * 3,
        scratch_shapes=[
            pltpu.VMEM(acts.shape, acts.dtype),
            pltpu.VMEM(out_grads.shape, out_grads.dtype),
            pltpu.VMEM(in_t.shape, in_t.dtype),
            pltpu.VMEM(out_t.shape, out_t.dtype),
            pltpu.VMEM(query_ids.shape, query_ids.dtype),
            pltpu.SemaphoreType.DMA((5 + len(g_cuts),)),
        ],
        compiler_params=pltpu.CompilerParams(vmem_limit_bytes=16 * 2**20),
        name="project",
    )(*[pltpu.with_memory_space_constraint(x, pltpu.HBM) for x in operands])


def sketch(mine, other, ids, rin):
    rout = mine.shape[0] - rin
    tok = mine.shape[1]
    groups = LANES // rin
    o_per = rout // groups

    def kernel(mine_ref, other_ref, ids_ref, out_ref):
        both = (mine_ref[...] + other_ref[...]).astype(jnp.bfloat16)
        left = both[0:rin]
        right = both[rin : rin + rout].astype(jnp.float32)
        member = lax.broadcasted_iota(jnp.int32, (E_DEV, tok), 0) == ids_ref[...]
        member = jnp.where(member, 1.0, 0.0)
        zero = jnp.zeros((rin, tok), jnp.bfloat16)
        columns, rows = [], []
        for g in range(groups):
            masked = [member * right[g * o_per + o : g * o_per + o + 1] for o in range(o_per)]
            columns.append(jnp.concatenate(masked, axis=0).astype(jnp.bfloat16))
            rows.append(jnp.concatenate([left if h == g else zero for h in range(groups)], axis=1))
        out_ref[...] = lax.dot_general(
            jnp.concatenate(columns, axis=1),
            jnp.concatenate(rows, axis=0),
            NT,
            preferred_element_type=jnp.float32,
        ).astype(jnp.bfloat16)

    return pl.pallas_call(
        kernel,
        out_shape=jax.ShapeDtypeStruct((o_per * E_DEV, LANES), jnp.bfloat16),
        compiler_params=pltpu.CompilerParams(vmem_limit_bytes=4 * 2**20),
        name="sketch",
    )(mine, other, ids)


def solve(blocks, pick):
    count = len(blocks)
    size = count * E_DEV
    k_size = blocks[0].shape[0] * LANES // E_DEV
    queries = pick.shape[1]
    group = 2

    def kernel(*refs):
        block_refs, pick_ref, out_ref = refs[:count], refs[count], refs[count + 1]

        def flat(ref):
            block = ref[...].astype(jnp.float32)
            cuts = [block[r : r + E_DEV] for r in range(0, block.shape[0], E_DEV)]
            return jnp.concatenate(cuts, axis=1)

        flats = [flat(ref) for ref in block_refs]
        every = jnp.concatenate(flats, axis=0).astype(jnp.bfloat16)
        twice = jnp.concatenate([every, every], axis=0)
        gram = lax.dot_general(every, twice, NT, preferred_element_type=jnp.float32)
        squares = sum(f * f for f in flats)
        squares = sum(squares[:, s : s + LANES] for s in range(0, k_size, LANES))
        total = jnp.sum(jnp.sum(squares, axis=0, keepdims=True), axis=1, keepdims=True)
        shape = (E_DEV, 2 * size)
        damping = jnp.broadcast_to(total * (0.1 / k_size), shape)
        row = lax.broadcasted_iota(jnp.int32, gram.shape, 0)
        lane = lax.broadcasted_iota(jnp.int32, gram.shape, 1)
        system = jnp.where(lane < size, jnp.where(row == lane, 1.0, 0.0), gram)
        table = [system[r : r + E_DEV] for r in range(0, size, E_DEV)]
        sub = lax.broadcasted_iota(jnp.int32, shape, 0)
        lane = lax.broadcasted_iota(jnp.int32, shape, 1)
        here = [sub == i for i in range(E_DEV)]

        def down(value, i):
            return jnp.broadcast_to(value[i : i + 1], shape)

        for first in range(0, count, group):
            own = range(group)
            base = size + first * E_DEV
            wide = [[jnp.broadcast_to(t[:, c : c + 1], shape) for c in range(base, base + group * E_DEV)] for t in table]
            rows = [
                table[first + k] + jnp.where(lane == sub + (base + k * E_DEV), damping, 0.0) for k in own
            ]
            cols = [
                [wide[first + k][j] + jnp.where(here[j % E_DEV], damping, 0.0) if j // E_DEV == k else wide[first + k][j]
                 for j in range(group * E_DEV)]
                for k in own
            ]
            scales = [jnp.zeros(shape, jnp.float32) for k in own]
            for i in range(group * E_DEV):
                which, at = i // E_DEV, i % E_DEV
                scale = 1.0 / down(cols[which][i], at)
                scales[which] = jnp.where(here[at], scale, scales[which])
                factor = [jnp.where(here[at], 0.0, cols[k][i]) if k == which else cols[k][i] for k in own]

                def clear(values):
                    line = down(values[which], at)
                    return [values[k] - (factor[k] * line) * scale for k in own]

                for j in range(i + 1, group * E_DEV):
                    fresh = clear([cols[k][j] for k in own])
                    for k in own:
                        cols[k][j] = fresh[k]
                rows = clear(rows)
            for k in own:
                table[first + k] = rows[k] * scales[k]
            lines = [down(table[first + j // E_DEV], j % E_DEV) for j in range(group * E_DEV)]
            for r in range(count):
                if not first <= r < first + group:
                    terms = [wide[r][j] * lines[j] for j in range(group * E_DEV)]
                    while len(terms) > 1:
                        terms = [x + y for x, y in zip(terms[::2], terms[1::2])]
                    table[r] = table[r] - terms[0]

        result = (jnp.where(sub == lane, 1.0, 0.0) - damping * table[0])[:, 0:size]
        high = result.astype(jnp.bfloat16).astype(jnp.float32)
        mid = (result - high).astype(jnp.bfloat16).astype(jnp.float32)
        parts = jnp.concatenate([high, mid, result - high - mid], axis=0).astype(jnp.bfloat16)
        rows = jnp.dot(parts, pick_ref[...], preferred_element_type=jnp.float32)
        out_ref[...] = rows[0:E_DEV] + (rows[E_DEV : 2 * E_DEV] + rows[2 * E_DEV : 3 * E_DEV])

    vmem = pl.BlockSpec(memory_space=pltpu.VMEM)
    return pl.pallas_call(
        kernel,
        out_shape=jax.ShapeDtypeStruct((E_DEV, queries), jnp.float32),
        in_specs=[vmem] * (count + 1),
        out_specs=vmem,
        compiler_params=pltpu.CompilerParams(vmem_limit_bytes=8 * 2**20),
        name="solve",
    )(*blocks, pick)


def fetch(value, step):
    moves = [(2 * i + c, 2 * to + c) for c in range(2) for i, to in enumerate(step[c])]
    return lax.ppermute(value, ("dp", "mp"), moves)


def swap(value):
    return lax.ppermute(value, "mp", [(0, 1), (1, 0)])


def local_small(acts, out_grads, in_proj, out_proj, example_ids, query_ids):
    count = lax.axis_size("dp")
    mine, ids, pick = project(
        acts, out_grads, in_proj.T, out_proj.T, example_ids, query_ids.reshape(1, -1), count
    )
    own = sketch(mine, swap(mine), ids, in_proj.shape[1])
    near = [fetch(own, step) for step in STEPS]
    far = [swap(block) for block in near[1:]]
    return solve([own] + near + far, pick).T


def chol_solve(factor, rhs):
    inner = lax.linalg.triangular_solve(factor, rhs, left_side=True, lower=True)
    return lax.linalg.triangular_solve(factor, inner, left_side=True, lower=True, transpose_a=True)


def local_large(acts, out_grads, in_proj, out_proj, example_ids, query_ids):
    part_in = jnp.dot(acts, in_proj, preferred_element_type=jnp.float32)
    part_out = jnp.dot(out_grads, out_proj, preferred_element_type=jnp.float32)
    full_in, full_out = lax.psum((part_in, part_out), "mp")
    left = full_in.astype(jnp.bfloat16)
    right = full_out.astype(jnp.bfloat16)
    tok_count = left.shape[0]
    rin_size = left.shape[1]
    rout_size = right.shape[1]
    k_size = rin_size * rout_size
    ids = example_ids[0]
    onehot = (ids[:, None] == jnp.arange(E_DEV, dtype=jnp.int32)[None, :]).astype(jnp.bfloat16)
    wide = (onehot[:, :, None] * left[:, None, :]).reshape(tok_count, E_DEV * rin_size)
    summed = lax.dot_general(
        right, wide, (((0,), (0,)), ((), ())), preferred_element_type=jnp.float32
    )
    local_sk = (
        summed.reshape(rout_size, E_DEV, rin_size)
        .transpose(1, 0, 2)
        .reshape(E_DEV, k_size)
        .astype(jnp.bfloat16)
    )
    every_sk = lax.all_gather(local_sk, "dp", axis=0, tiled=True)
    gram = lax.dot_general(
        every_sk, every_sk, (((0,), (0,)), ((), ())), preferred_element_type=jnp.float32
    )
    local_f32 = local_sk.astype(jnp.float32)
    total_sq = lax.psum(jnp.sum(local_f32 * local_f32), "dp")
    damping = 0.1 * total_sq / k_size
    damped = gram + damping * jnp.eye(k_size, dtype=jnp.float32)
    factor = jnp.linalg.cholesky(damped)
    queried = jnp.take(every_sk, query_ids, axis=0).astype(jnp.float32)
    precond = chol_solve(factor, queried.T)
    return lax.dot_general(
        precond, local_f32, (((0,), (1,)), ((), ())), precision=lax.Precision.HIGHEST
    )


def solution(mesh):
    in_specs = (
        P(("groups", "dp"), "mp"),
        P(("groups", "dp"), "mp"),
        P("mp", None),
        P("mp", None),
        P(("groups", "dp"), None),
        P(("groups", "mp")),
    )
    out_specs = P(("groups", "mp"), "dp")
    small = mesh.shape["dp"] == 8 and mesh.shape["mp"] == 2
    local = local_small if small else local_large
    return jax.shard_map(local, mesh=mesh, in_specs=in_specs, out_specs=out_specs, check_vma=False)
```

```python
import jax
import jax.numpy as jnp
from jax import lax
from jax.experimental import pallas as pl
from jax.experimental.pallas import tpu as pltpu
from jax.sharding import PartitionSpec as P

E_DEV = 8
LANES = 128
NT = (((1,), (1,)), ((), ()))
STEPS = (
    (7, 6, 1, 0, 3, 2, 8, 9, 15, 14, 13, 12, 10, 11, 5, 4),
    (11, 15, 13, 4, 9, 1, 10, 0, 3, 7, 14, 2, 5, 6, 12, 8),
    (9, 13, 15, 10, 14, 6, 2, 4, 12, 5, 8, 1, 3, 0, 7, 11),
    (5, 3, 9, 6, 13, 10, 15, 12, 11, 0, 4, 7, 14, 8, 1, 2),
)


def places(device):
    blocks = [device // 2]
    blocks += [step.index(device) // 2 for step in STEPS]
    blocks += [step.index(device ^ 1) // 2 for step in STEPS[1:]]
    return sum(blocks.index(owner) << (4 * owner) for owner in range(len(blocks)))


def chunks(size, parts):
    per = -(-size // (parts * LANES)) * LANES
    starts = range(0, size, per)
    return [(s, min(per, size - s)) for s in starts]


def project(acts, out_grads, in_t, out_t, example_ids, query_ids, count):
    rin, rout = in_t.shape[0], out_t.shape[0]
    tok = acts.shape[0]
    queries = query_ids.shape[1]
    g_cuts = chunks(out_grads.shape[1], 2)

    def kernel(a_hbm, g_hbm, i_hbm, o_hbm, e_hbm, q_hbm, out_ref, e_ref, pick_ref, a_v, g_v, i_v, o_v, q_v, sems):
        copies = []

        def start(src, dst):
            copy = pltpu.make_async_copy(src, dst, sems.at[len(copies)])
            copy.start()
            copies.append(copy)
            return copy

        q_copy = start(q_hbm, q_v)
        i_copy = start(i_hbm, i_v)
        a_copy = start(a_hbm, a_v)
        o_copy = start(o_hbm, o_v)
        g_copies = [start(g_hbm.at[:, pl.ds(s, n)], g_v.at[:, pl.ds(s, n)]) for s, n in g_cuts]
        e_copy = start(e_hbm, e_ref)
        q_copy.wait()
        device = lax.axis_index("dp") * 2 + lax.axis_index("mp")
        code = jnp.int32(0)
        for n in range(2 * count):
            bits = places(n)
            code = jnp.where(device == n, bits - (bits >> 31 << 32), code)
        ids = q_v[...]
        spot = ((code >> (ids // E_DEV * 4)) & 7) * E_DEV + ids % E_DEV
        row = lax.broadcasted_iota(jnp.int32, pick_ref.shape, 0)
        pick_ref[...] = jnp.where(row == spot, 1.0, 0.0).astype(jnp.bfloat16)
        i_copy.wait()
        a_copy.wait()
        out_ref[0:rin, :] = lax.dot_general(i_v[...], a_v[...], NT, preferred_element_type=jnp.float32)
        o_copy.wait()
        total = None
        for copy, (s, n) in zip(g_copies, g_cuts):
            copy.wait()
            term = lax.dot_general(o_v[:, s : s + n], g_v[:, s : s + n], NT, preferred_element_type=jnp.float32)
            total = term if total is None else total + term
        out_ref[rin : rin + rout, :] = total
        e_copy.wait()

    hbm = pl.BlockSpec(memory_space=pltpu.HBM)
    vmem = pl.BlockSpec(memory_space=pltpu.VMEM)
    operands = (acts, out_grads, in_t, out_t, example_ids, query_ids)
    return pl.pallas_call(
        kernel,
        out_shape=[
            jax.ShapeDtypeStruct((rin + rout, tok), jnp.float32),
            jax.ShapeDtypeStruct(example_ids.shape, example_ids.dtype),
            jax.ShapeDtypeStruct((count * E_DEV, queries), jnp.bfloat16),
        ],
        in_specs=[hbm] * 6,
        out_specs=[vmem] * 3,
        scratch_shapes=[
            pltpu.VMEM(acts.shape, acts.dtype),
            pltpu.VMEM(out_grads.shape, out_grads.dtype),
            pltpu.VMEM(in_t.shape, in_t.dtype),
            pltpu.VMEM(out_t.shape, out_t.dtype),
            pltpu.VMEM(query_ids.shape, query_ids.dtype),
            pltpu.SemaphoreType.DMA((5 + len(g_cuts),)),
        ],
        compiler_params=pltpu.CompilerParams(vmem_limit_bytes=16 * 2**20),
        name="project",
    )(*[pltpu.with_memory_space_constraint(x, pltpu.HBM) for x in operands])


def sketch(mine, other, ids, rin):
    rout = mine.shape[0] - rin
    tok = mine.shape[1]
    groups = LANES // rin
    o_per = rout // groups

    def kernel(mine_ref, other_ref, ids_ref, out_ref):
        both = (mine_ref[...] + other_ref[...]).astype(jnp.bfloat16)
        left = both[0:rin]
        right = both[rin : rin + rout].astype(jnp.float32)
        member = lax.broadcasted_iota(jnp.int32, (E_DEV, tok), 0) == ids_ref[...]
        member = jnp.where(member, 1.0, 0.0)
        zero = jnp.zeros((rin, tok), jnp.bfloat16)
        columns, rows = [], []
        for g in range(groups):
            masked = [member * right[g * o_per + o : g * o_per + o + 1] for o in range(o_per)]
            columns.append(jnp.concatenate(masked, axis=0).astype(jnp.bfloat16))
            rows.append(jnp.concatenate([left if h == g else zero for h in range(groups)], axis=1))
        out_ref[...] = lax.dot_general(
            jnp.concatenate(columns, axis=1),
            jnp.concatenate(rows, axis=0),
            NT,
            preferred_element_type=jnp.float32,
        ).astype(jnp.bfloat16)

    return pl.pallas_call(
        kernel,
        out_shape=jax.ShapeDtypeStruct((o_per * E_DEV, LANES), jnp.bfloat16),
        compiler_params=pltpu.CompilerParams(vmem_limit_bytes=4 * 2**20),
        name="sketch",
    )(mine, other, ids)


def solve(blocks, pick):
    count = len(blocks)
    size = count * E_DEV
    k_size = blocks[0].shape[0] * LANES // E_DEV
    queries = pick.shape[1]
    group = 2
    span = group * E_DEV

    def kernel(*refs):
        block_refs, pick_ref, out_ref, basis = refs[:count], refs[count], refs[count + 1], refs[count + 2]

        def flat(ref):
            block = ref[...].astype(jnp.float32)
            cuts = [block[r : r + E_DEV] for r in range(0, block.shape[0], E_DEV)]
            return jnp.concatenate(cuts, axis=1)

        flats = [flat(ref) for ref in block_refs]
        every = jnp.concatenate(flats, axis=0).astype(jnp.bfloat16)
        twice = jnp.concatenate([every, every], axis=0)
        gram = lax.dot_general(every, twice, NT, preferred_element_type=jnp.float32)
        squares = sum(f * f for f in flats)
        squares = sum(squares[:, s : s + LANES] for s in range(0, k_size, LANES))
        total = jnp.sum(jnp.sum(squares, axis=0, keepdims=True), axis=1, keepdims=True)
        shape = (E_DEV, 2 * size)
        damping = jnp.broadcast_to(total * (0.1 / k_size), shape)
        row = lax.broadcasted_iota(jnp.int32, gram.shape, 0)
        lane = lax.broadcasted_iota(jnp.int32, gram.shape, 1)
        diagonal = row == lane
        system = jnp.where(lane < size, jnp.where(diagonal, 1.0, 0.0), gram)
        table = [system[r : r + E_DEV] for r in range(0, size, E_DEV)]
        sub = lax.broadcasted_iota(jnp.int32, shape, 0)
        lane = lax.broadcasted_iota(jnp.int32, shape, 1)
        here = [sub == i for i in range(E_DEV)]
        norms = jnp.sum(jnp.where(diagonal, gram, 0.0), axis=1, keepdims=True)
        norms = [jnp.broadcast_to(norms[r : r + E_DEV], shape) for r in range(0, size, E_DEV)]
        spread = jnp.zeros(shape, jnp.float32)

        def down(value, i):
            return jnp.broadcast_to(value[i : i + 1], shape)

        for first in range(0, count, group):
            own = range(group)
            base = size + first * E_DEV
            wide = [[jnp.broadcast_to(t[:, c : c + 1], shape) for c in range(base, base + span)] for t in table]
            rows = [table[first + k] + jnp.where(lane == sub + (base + k * E_DEV), damping, 0.0) for k in own]
            cols = [list(wide[first + k]) for k in own]
            for j in range(span):
                k = j // E_DEV
                cols[k][j] = cols[k][j] + jnp.where(here[j % E_DEV], damping, 0.0)
            scalings = []
            for i in range(0, span, 2):
                which, at = i // E_DEV, i % E_DEV
                p, q = down(cols[which][i], at), down(cols[which][i + 1], at)
                s, t = down(cols[which][i], at + 1), down(cols[which][i + 1], at + 1)
                inverse = 1.0 / (p * t - q * s)
                scalings.append((t * inverse, q * inverse, p * inverse, s * inverse))
                norm = norms[first + which]
                spread = spread + (down(norm, at) * scalings[-1][0] + down(norm, at + 1) * scalings[-1][2])
                factors = []
                for k in own:
                    x, y = cols[k][i], cols[k][i + 1]
                    pair = (x * t - y * s, y * p - x * q)
                    if k == which:
                        pair = [jnp.where(here[at] | here[at + 1], 0.0, f) for f in pair]
                    factors.append([f * inverse for f in pair])

                def clear(values):
                    upper, lower = down(values[which], at), down(values[which], at + 1)
                    return [values[k] - (factors[k][0] * upper + factors[k][1] * lower) for k in own]

                for j in range(i + 2, span):
                    fresh = clear([cols[k][j] for k in own])
                    for k in own:
                        cols[k][j] = fresh[k]
                rows = clear(rows)
            for k in own:
                scaled = rows[k]
                for at in range(0, E_DEV, 2):
                    a, b, c, d = scalings[(k * E_DEV + at) // 2]
                    upper, lower = down(rows[k], at), down(rows[k], at + 1)
                    scaled = jnp.where(here[at], a * upper - b * lower, scaled)
                    scaled = jnp.where(here[at + 1], c * lower - d * upper, scaled)
                table[first + k] = scaled
            lines = [down(table[first + j // E_DEV], j % E_DEV) for j in range(span)]
            for r in range(count):
                if not first <= r < first + group:
                    terms = [wide[r][j] * lines[j] for j in range(span)]
                    while len(terms) > 1:
                        terms = [x + y for x, y in zip(terms[::2], terms[1::2])]
                    table[r] = table[r] - terms[0]

        eye = jnp.where(sub == lane, 1.0, 0.0)

        def picked(result):
            result = result[:, 0:size]
            high = result.astype(jnp.bfloat16).astype(jnp.float32)
            mid = (result - high).astype(jnp.bfloat16).astype(jnp.float32)
            parts = jnp.concatenate([high, mid, result - high - mid], axis=0).astype(jnp.bfloat16)
            found = jnp.dot(parts, pick_ref[...], preferred_element_type=jnp.float32)
            return found[0:E_DEV] + (found[E_DEV : 2 * E_DEV] + found[2 * E_DEV : 3 * E_DEV])

        out_ref[...] = picked(eye - damping * table[0])

        @pl.when(spread[0, 0] > 4.0 * size)
        def _():
            for k, ref in enumerate(block_refs):
                basis[k * E_DEV : (k + 1) * E_DEV, 0:k_size] = flat(ref)
            root = jnp.sqrt(damping[0:1, :])
            basis[:, k_size : k_size + 2 * size] = jnp.where(diagonal, jnp.broadcast_to(root, gram.shape), 0.0)
            number = lax.broadcasted_iota(jnp.int32, (size, 1), 0)

            def step(i, carry):
                line = basis[pl.ds(i, 1), :]
                line = line / jnp.sqrt(jnp.sum(line * line, axis=1, keepdims=True))
                everything = basis[...]
                part = jnp.sum(everything * line, axis=1, keepdims=True)
                part = jnp.where(number > i, part, 0.0)
                basis[...] = jnp.where(number == i, line, everything - part * line)
                return carry

            lax.fori_loop(0, size, step, 0)
            tail = basis[:, k_size : k_size + 2 * size]
            rest = lax.dot_general(
                tail, tail, (((0,), (0,)), ((), ())), precision=lax.Precision.HIGHEST, preferred_element_type=jnp.float32
            )
            out_ref[...] = picked(eye - rest[0:E_DEV])

    vmem = pl.BlockSpec(memory_space=pltpu.VMEM)
    return pl.pallas_call(
        kernel,
        out_shape=jax.ShapeDtypeStruct((E_DEV, queries), jnp.float32),
        in_specs=[vmem] * (count + 1),
        out_specs=vmem,
        scratch_shapes=[pltpu.VMEM((size, k_size + 2 * size), jnp.float32)],
        compiler_params=pltpu.CompilerParams(vmem_limit_bytes=8 * 2**20),
        name="solve",
    )(*blocks, pick)


def fetch(value, step):
    return lax.ppermute(value, ("dp", "mp"), list(enumerate(step)))


def swap(value):
    return lax.ppermute(value, "mp", [(0, 1), (1, 0)])


def local_small(acts, out_grads, in_proj, out_proj, example_ids, query_ids):
    count = lax.axis_size("dp")
    mine, ids, pick = project(
        acts, out_grads, in_proj.T, out_proj.T, example_ids, query_ids.reshape(1, -1), count
    )
    own = sketch(mine, swap(mine), ids, in_proj.shape[1])
    near = [fetch(own, step) for step in STEPS]
    far = [swap(block) for block in near[1:]]
    return solve([own] + near + far, pick).T


def chol_solve(factor, rhs):
    inner = lax.linalg.triangular_solve(factor, rhs, left_side=True, lower=True)
    return lax.linalg.triangular_solve(factor, inner, left_side=True, lower=True, transpose_a=True)


def local_large(acts, out_grads, in_proj, out_proj, example_ids, query_ids):
    part_in = jnp.dot(acts, in_proj, preferred_element_type=jnp.float32)
    part_out = jnp.dot(out_grads, out_proj, preferred_element_type=jnp.float32)
    full_in, full_out = lax.psum((part_in, part_out), "mp")
    left = full_in.astype(jnp.bfloat16)
    right = full_out.astype(jnp.bfloat16)
    tok_count = left.shape[0]
    rin_size = left.shape[1]
    rout_size = right.shape[1]
    k_size = rin_size * rout_size
    ids = example_ids[0]
    onehot = (ids[:, None] == jnp.arange(E_DEV, dtype=jnp.int32)[None, :]).astype(jnp.bfloat16)
    wide = (onehot[:, :, None] * left[:, None, :]).reshape(tok_count, E_DEV * rin_size)
    summed = lax.dot_general(
        right, wide, (((0,), (0,)), ((), ())), preferred_element_type=jnp.float32
    )
    local_sk = (
        summed.reshape(rout_size, E_DEV, rin_size)
        .transpose(1, 0, 2)
        .reshape(E_DEV, k_size)
        .astype(jnp.bfloat16)
    )
    every_sk = lax.all_gather(local_sk, "dp", axis=0, tiled=True)
    gram = lax.dot_general(
        every_sk, every_sk, (((0,), (0,)), ((), ())), preferred_element_type=jnp.float32
    )
    local_f32 = local_sk.astype(jnp.float32)
    total_sq = lax.psum(jnp.sum(local_f32 * local_f32), "dp")
    damping = 0.1 * total_sq / k_size
    damped = gram + damping * jnp.eye(k_size, dtype=jnp.float32)
    factor = jnp.linalg.cholesky(damped)
    queried = jnp.take(every_sk, query_ids, axis=0).astype(jnp.float32)
    precond = chol_solve(factor, queried.T)
    return lax.dot_general(
        precond, local_f32, (((0,), (1,)), ((), ())), precision=lax.Precision.HIGHEST
    )


def solution(mesh):
    in_specs = (
        P(("groups", "dp"), "mp"),
        P(("groups", "dp"), "mp"),
        P("mp", None),
        P("mp", None),
        P(("groups", "dp"), None),
        P(("groups", "mp")),
    )
    out_specs = P(("groups", "mp"), "dp")
    small = mesh.shape["dp"] == 8 and mesh.shape["mp"] == 2
    local = local_small if small else local_large
    return jax.shard_map(local, mesh=mesh, in_specs=in_specs, out_specs=out_specs, check_vma=False)
```

```python
import jax
import jax.numpy as jnp
from jax import lax
from jax.experimental import pallas as pl
from jax.experimental.pallas import tpu as pltpu
from jax.sharding import PartitionSpec as P

E_DEV = 8
LANES = 128
NT = (((1,), (1,)), ((), ()))
STEPS = (
    (9, 8, 13, 12, 1, 0, 15, 14, 6, 7, 5, 4, 11, 10, 3, 2),
    (13, 14, 7, 0, 10, 3, 8, 2, 5, 1, 6, 12, 4, 15, 9, 11),
    (11, 5, 10, 9, 13, 15, 12, 0, 2, 14, 8, 3, 6, 1, 7, 4),
    (7, 3, 4, 14, 8, 6, 10, 5, 12, 11, 15, 0, 2, 9, 13, 1),
)


def places(device):
    blocks = [device // 2]
    blocks += [step.index(device) // 2 for step in STEPS]
    blocks += [step.index(device ^ 1) // 2 for step in STEPS[1:]]
    return sum(blocks.index(owner) << (4 * owner) for owner in range(len(blocks)))


def chunks(size, parts):
    per = -(-size // (parts * LANES)) * LANES
    starts = range(0, size, per)
    return [(s, min(per, size - s)) for s in starts]


def project(acts, out_grads, in_t, out_t, example_ids, query_ids, count):
    rin, rout = in_t.shape[0], out_t.shape[0]
    tok = acts.shape[0]
    queries = query_ids.shape[1]
    g_cuts = chunks(out_grads.shape[1], 2)

    def kernel(a_hbm, g_hbm, i_hbm, o_hbm, e_hbm, q_hbm, out_ref, e_ref, pick_ref, a_v, g_v, i_v, o_v, q_v, sems):
        copies = []

        def start(src, dst):
            copy = pltpu.make_async_copy(src, dst, sems.at[len(copies)])
            copy.start()
            copies.append(copy)
            return copy

        q_copy = start(q_hbm, q_v)
        i_copy = start(i_hbm, i_v)
        a_copy = start(a_hbm, a_v)
        o_copy = start(o_hbm, o_v)
        g_copies = [start(g_hbm.at[:, pl.ds(s, n)], g_v.at[:, pl.ds(s, n)]) for s, n in g_cuts]
        e_copy = start(e_hbm, e_ref)
        q_copy.wait()
        device = lax.axis_index("dp") * 2 + lax.axis_index("mp")
        code = jnp.int32(0)
        for n in range(2 * count):
            bits = places(n)
            code = jnp.where(device == n, bits - (bits >> 31 << 32), code)
        ids = q_v[...]
        spot = ((code >> (ids // E_DEV * 4)) & 7) * E_DEV + ids % E_DEV
        row = lax.broadcasted_iota(jnp.int32, pick_ref.shape, 0)
        pick_ref[...] = jnp.where(row == spot, 1.0, 0.0).astype(jnp.bfloat16)
        i_copy.wait()
        a_copy.wait()
        out_ref[0:rin, :] = lax.dot_general(i_v[...], a_v[...], NT, preferred_element_type=jnp.float32)
        o_copy.wait()
        total = None
        for copy, (s, n) in zip(g_copies, g_cuts):
            copy.wait()
            term = lax.dot_general(o_v[:, s : s + n], g_v[:, s : s + n], NT, preferred_element_type=jnp.float32)
            total = term if total is None else total + term
        out_ref[rin : rin + rout, :] = total
        e_copy.wait()

    hbm = pl.BlockSpec(memory_space=pltpu.HBM)
    vmem = pl.BlockSpec(memory_space=pltpu.VMEM)
    operands = (acts, out_grads, in_t, out_t, example_ids, query_ids)
    return pl.pallas_call(
        kernel,
        out_shape=[
            jax.ShapeDtypeStruct((rin + rout, tok), jnp.float32),
            jax.ShapeDtypeStruct(example_ids.shape, example_ids.dtype),
            jax.ShapeDtypeStruct((count * E_DEV, queries), jnp.bfloat16),
        ],
        in_specs=[hbm] * 6,
        out_specs=[vmem] * 3,
        scratch_shapes=[
            pltpu.VMEM(acts.shape, acts.dtype),
            pltpu.VMEM(out_grads.shape, out_grads.dtype),
            pltpu.VMEM(in_t.shape, in_t.dtype),
            pltpu.VMEM(out_t.shape, out_t.dtype),
            pltpu.VMEM(query_ids.shape, query_ids.dtype),
            pltpu.SemaphoreType.DMA((5 + len(g_cuts),)),
        ],
        compiler_params=pltpu.CompilerParams(vmem_limit_bytes=16 * 2**20),
        name="project",
    )(*[pltpu.with_memory_space_constraint(x, pltpu.HBM) for x in operands])


def sketch(mine, other, ids, rin):
    rout = mine.shape[0] - rin
    tok = mine.shape[1]
    groups = LANES // rin
    o_per = rout // groups

    def kernel(mine_ref, other_ref, ids_ref, out_ref):
        both = (mine_ref[...] + other_ref[...]).astype(jnp.bfloat16)
        left = both[0:rin]
        right = both[rin : rin + rout].astype(jnp.float32)
        member = lax.broadcasted_iota(jnp.int32, (E_DEV, tok), 0) == ids_ref[...]
        member = jnp.where(member, 1.0, 0.0)
        zero = jnp.zeros((rin, tok), jnp.bfloat16)
        columns, rows = [], []
        for g in range(groups):
            masked = [member * right[g * o_per + o : g * o_per + o + 1] for o in range(o_per)]
            columns.append(jnp.concatenate(masked, axis=0).astype(jnp.bfloat16))
            rows.append(jnp.concatenate([left if h == g else zero for h in range(groups)], axis=1))
        out_ref[...] = lax.dot_general(
            jnp.concatenate(columns, axis=1),
            jnp.concatenate(rows, axis=0),
            NT,
            preferred_element_type=jnp.float32,
        ).astype(jnp.bfloat16)

    return pl.pallas_call(
        kernel,
        out_shape=jax.ShapeDtypeStruct((o_per * E_DEV, LANES), jnp.bfloat16),
        compiler_params=pltpu.CompilerParams(vmem_limit_bytes=4 * 2**20),
        name="sketch",
    )(mine, other, ids)


def solve(blocks, pick):
    count = len(blocks)
    size = count * E_DEV
    k_size = blocks[0].shape[0] * LANES // E_DEV
    queries = pick.shape[1]
    group = 2
    span = group * E_DEV

    def kernel(*refs):
        block_refs, pick_ref, out_ref, basis = refs[:count], refs[count], refs[count + 1], refs[count + 2]

        def flat(ref):
            block = ref[...].astype(jnp.float32)
            cuts = [block[r : r + E_DEV] for r in range(0, block.shape[0], E_DEV)]
            return jnp.concatenate(cuts, axis=1)

        flats = [flat(ref) for ref in block_refs]
        every = jnp.concatenate(flats, axis=0).astype(jnp.bfloat16)
        twice = jnp.concatenate([every, every], axis=0)
        gram = lax.dot_general(every, twice, NT, preferred_element_type=jnp.float32)
        squares = sum(f * f for f in flats)
        squares = sum(squares[:, s : s + LANES] for s in range(0, k_size, LANES))
        total = jnp.sum(jnp.sum(squares, axis=0, keepdims=True), axis=1, keepdims=True)
        shape = (E_DEV, 2 * size)
        damping = jnp.broadcast_to(total * (0.1 / k_size), shape)
        row = lax.broadcasted_iota(jnp.int32, gram.shape, 0)
        lane = lax.broadcasted_iota(jnp.int32, gram.shape, 1)
        diagonal = row == lane
        system = jnp.where(lane < size, jnp.where(diagonal, 1.0, 0.0), gram)
        table = [system[r : r + E_DEV] for r in range(0, size, E_DEV)]
        sub = lax.broadcasted_iota(jnp.int32, shape, 0)
        lane = lax.broadcasted_iota(jnp.int32, shape, 1)
        here = [sub == i for i in range(E_DEV)]
        norms = jnp.sum(jnp.where(diagonal, gram, 0.0), axis=1, keepdims=True)
        norms = [jnp.broadcast_to(norms[r : r + E_DEV], shape) for r in range(0, size, E_DEV)]
        spread = jnp.zeros(shape, jnp.float32)

        def down(value, i):
            return jnp.broadcast_to(value[i : i + 1], shape)

        for first in range(0, count, group):
            own = range(group)
            base = size + first * E_DEV
            wide = [[jnp.broadcast_to(t[:, c : c + 1], shape) for c in range(base, base + span)] for t in table]
            rows = [table[first + k] + jnp.where(lane == sub + (base + k * E_DEV), damping, 0.0) for k in own]
            cols = [list(wide[first + k]) for k in own]
            for j in range(span):
                k = j // E_DEV
                cols[k][j] = cols[k][j] + jnp.where(here[j % E_DEV], damping, 0.0)
            scalings = []
            for i in range(0, span, 2):
                which, at = i // E_DEV, i % E_DEV
                p, q = down(cols[which][i], at), down(cols[which][i + 1], at)
                s, t = down(cols[which][i], at + 1), down(cols[which][i + 1], at + 1)
                inverse = 1.0 / (p * t - q * s)
                scalings.append((t * inverse, q * inverse, p * inverse, s * inverse))
                norm = norms[first + which]
                spread = spread + jnp.abs(down(norm, at) * scalings[-1][0]) + jnp.abs(down(norm, at + 1) * scalings[-1][2])
                factors = []
                for k in own:
                    x, y = cols[k][i], cols[k][i + 1]
                    pair = (x * t - y * s, y * p - x * q)
                    if k == which:
                        pair = [jnp.where(here[at] | here[at + 1], 0.0, f) for f in pair]
                    factors.append([f * inverse for f in pair])

                def clear(values):
                    upper, lower = down(values[which], at), down(values[which], at + 1)
                    return [values[k] - (factors[k][0] * upper + factors[k][1] * lower) for k in own]

                for j in range(i + 2, span):
                    fresh = clear([cols[k][j] for k in own])
                    for k in own:
                        cols[k][j] = fresh[k]
                rows = clear(rows)
            for k in own:
                scaled = rows[k]
                for at in range(0, E_DEV, 2):
                    a, b, c, d = scalings[(k * E_DEV + at) // 2]
                    upper, lower = down(rows[k], at), down(rows[k], at + 1)
                    scaled = jnp.where(here[at], a * upper - b * lower, scaled)
                    scaled = jnp.where(here[at + 1], c * lower - d * upper, scaled)
                table[first + k] = scaled
            lines = [down(table[first + j // E_DEV], j % E_DEV) for j in range(span)]
            for r in range(count):
                if not first <= r < first + group:
                    terms = [wide[r][j] * lines[j] for j in range(span)]
                    while len(terms) > 1:
                        terms = [x + y for x, y in zip(terms[::2], terms[1::2])]
                    table[r] = table[r] - terms[0]

        eye = jnp.where(sub == lane, 1.0, 0.0)

        def picked(result):
            result = result[:, 0:size]
            high = result.astype(jnp.bfloat16).astype(jnp.float32)
            mid = (result - high).astype(jnp.bfloat16).astype(jnp.float32)
            parts = jnp.concatenate([high, mid, result - high - mid], axis=0).astype(jnp.bfloat16)
            found = jnp.dot(parts, pick_ref[...], preferred_element_type=jnp.float32)
            return found[0:E_DEV] + (found[E_DEV : 2 * E_DEV] + found[2 * E_DEV : 3 * E_DEV])

        out_ref[...] = picked(eye - damping * table[0])

        @pl.when(jnp.logical_not(spread[0, 0] <= 4.0 * size))
        def _():
            for k, ref in enumerate(block_refs):
                basis[k * E_DEV : (k + 1) * E_DEV, 0:k_size] = flat(ref)
            root = jnp.sqrt(damping[0:1, :])
            basis[:, k_size : k_size + 2 * size] = jnp.where(diagonal, jnp.broadcast_to(root, gram.shape), 0.0)
            number = lax.broadcasted_iota(jnp.int32, (size, 1), 0)

            def step(i, carry):
                line = basis[pl.ds(i, 1), :]
                line = line / jnp.sqrt(jnp.sum(line * line, axis=1, keepdims=True))
                everything = basis[...]
                part = jnp.sum(everything * line, axis=1, keepdims=True)
                part = jnp.where(number > i, part, 0.0)
                basis[...] = jnp.where(number == i, line, everything - part * line)
                return carry

            lax.fori_loop(0, size, step, 0)
            tail = basis[:, k_size : k_size + 2 * size]
            rest = lax.dot_general(
                tail, tail, (((0,), (0,)), ((), ())), precision=lax.Precision.HIGHEST, preferred_element_type=jnp.float32
            )
            out_ref[...] = picked(eye - rest[0:E_DEV])

    vmem = pl.BlockSpec(memory_space=pltpu.VMEM)
    return pl.pallas_call(
        kernel,
        out_shape=jax.ShapeDtypeStruct((E_DEV, queries), jnp.float32),
        in_specs=[vmem] * (count + 1),
        out_specs=vmem,
        scratch_shapes=[pltpu.VMEM((size, k_size + 2 * size), jnp.float32)],
        compiler_params=pltpu.CompilerParams(vmem_limit_bytes=8 * 2**20),
        name="solve",
    )(*blocks, pick)


def fetch(value, step):
    return lax.ppermute(value, ("dp", "mp"), list(enumerate(step)))


def swap(value):
    return lax.ppermute(value, "mp", [(0, 1), (1, 0)])


def local_small(acts, out_grads, in_proj, out_proj, example_ids, query_ids):
    count = lax.axis_size("dp")
    mine, ids, pick = project(
        acts, out_grads, in_proj.T, out_proj.T, example_ids, query_ids.reshape(1, -1), count
    )
    own = sketch(mine, swap(mine), ids, in_proj.shape[1])
    near = [fetch(own, step) for step in STEPS]
    far = [swap(block) for block in near[1:]]
    return solve([own] + near + far, pick).T


def chol_solve(factor, rhs):
    inner = lax.linalg.triangular_solve(factor, rhs, left_side=True, lower=True)
    return lax.linalg.triangular_solve(factor, inner, left_side=True, lower=True, transpose_a=True)


def local_large(acts, out_grads, in_proj, out_proj, example_ids, query_ids):
    part_in = jnp.dot(acts, in_proj, preferred_element_type=jnp.float32)
    part_out = jnp.dot(out_grads, out_proj, preferred_element_type=jnp.float32)
    full_in, full_out = lax.psum((part_in, part_out), "mp")
    left = full_in.astype(jnp.bfloat16)
    right = full_out.astype(jnp.bfloat16)
    tok_count = left.shape[0]
    rin_size = left.shape[1]
    rout_size = right.shape[1]
    k_size = rin_size * rout_size
    ids = example_ids[0]
    onehot = (ids[:, None] == jnp.arange(E_DEV, dtype=jnp.int32)[None, :]).astype(jnp.bfloat16)
    wide = (onehot[:, :, None] * left[:, None, :]).reshape(tok_count, E_DEV * rin_size)
    summed = lax.dot_general(
        right, wide, (((0,), (0,)), ((), ())), preferred_element_type=jnp.float32
    )
    local_sk = (
        summed.reshape(rout_size, E_DEV, rin_size)
        .transpose(1, 0, 2)
        .reshape(E_DEV, k_size)
        .astype(jnp.bfloat16)
    )
    every_sk = lax.all_gather(local_sk, "dp", axis=0, tiled=True)
    gram = lax.dot_general(
        every_sk, every_sk, (((0,), (0,)), ((), ())), preferred_element_type=jnp.float32
    )
    local_f32 = local_sk.astype(jnp.float32)
    total_sq = lax.psum(jnp.sum(local_f32 * local_f32), "dp")
    damping = 0.1 * total_sq / k_size
    damped = gram + damping * jnp.eye(k_size, dtype=jnp.float32)
    factor = jnp.linalg.cholesky(damped)
    queried = jnp.take(every_sk, query_ids, axis=0).astype(jnp.float32)
    precond = chol_solve(factor, queried.T)
    return lax.dot_general(
        precond, local_f32, (((0,), (1,)), ((), ())), precision=lax.Precision.HIGHEST
    )


def solution(mesh):
    in_specs = (
        P(("groups", "dp"), "mp"),
        P(("groups", "dp"), "mp"),
        P("mp", None),
        P("mp", None),
        P(("groups", "dp"), None),
        P(("groups", "mp")),
    )
    out_specs = P(("groups", "mp"), "dp")
    small = mesh.shape["dp"] == 8 and mesh.shape["mp"] == 2
    local = local_small if small else local_large
    return jax.shard_map(local, mesh=mesh, in_specs=in_specs, out_specs=out_specs, check_vma=False)
```

```python
import jax
import jax.numpy as jnp
from jax import lax
from jax.experimental import pallas as pl
from jax.experimental.pallas import tpu as pltpu
from jax.sharding import PartitionSpec as P

E_DEV = 8
LANES = 128
NT = (((1,), (1,)), ((), ()))
STEPS = (
    (9, 8, 13, 12, 1, 0, 15, 14, 6, 7, 5, 4, 11, 10, 3, 2),
    (13, 14, 7, 0, 10, 3, 8, 2, 5, 1, 6, 12, 4, 15, 9, 11),
    (11, 5, 10, 9, 13, 15, 12, 0, 2, 14, 8, 3, 6, 1, 7, 4),
    (7, 3, 4, 14, 8, 6, 10, 5, 12, 11, 15, 0, 2, 9, 13, 1),
)


def places(device):
    blocks = [device // 2]
    blocks += [step.index(device) // 2 for step in STEPS]
    blocks += [step.index(device ^ 1) // 2 for step in STEPS[1:]]
    return sum(blocks.index(owner) << (4 * owner) for owner in range(len(blocks)))


def chunks(size, parts):
    per = -(-size // (parts * LANES)) * LANES
    starts = range(0, size, per)
    return [(s, min(per, size - s)) for s in starts]


def project(acts, out_grads, in_t, out_t, example_ids, query_ids, count):
    rin, rout = in_t.shape[0], out_t.shape[0]
    tok = acts.shape[0]
    queries = query_ids.shape[1]
    g_cuts = chunks(out_grads.shape[1], 2)

    def kernel(a_hbm, g_hbm, i_hbm, o_hbm, e_hbm, q_hbm, out_ref, e_ref, pick_ref, a_v, g_v, i_v, o_v, q_v, sems):
        copies = []

        def start(src, dst):
            copy = pltpu.make_async_copy(src, dst, sems.at[len(copies)])
            copy.start()
            copies.append(copy)
            return copy

        q_copy = start(q_hbm, q_v)
        i_copy = start(i_hbm, i_v)
        a_copy = start(a_hbm, a_v)
        o_copy = start(o_hbm, o_v)
        g_copies = [start(g_hbm.at[:, pl.ds(s, n)], g_v.at[:, pl.ds(s, n)]) for s, n in g_cuts]
        e_copy = start(e_hbm, e_ref)
        q_copy.wait()
        device = lax.axis_index("dp") * 2 + lax.axis_index("mp")
        code = jnp.int32(0)
        for n in range(2 * count):
            bits = places(n)
            code = jnp.where(device == n, bits - (bits >> 31 << 32), code)
        ids = q_v[...]
        spot = ((code >> (ids // E_DEV * 4)) & 7) * E_DEV + ids % E_DEV
        row = lax.broadcasted_iota(jnp.int32, pick_ref.shape, 0)
        pick_ref[...] = jnp.where(row == spot, 1.0, 0.0).astype(jnp.bfloat16)
        i_copy.wait()
        a_copy.wait()
        out_ref[0:rin, :] = lax.dot_general(i_v[...], a_v[...], NT, preferred_element_type=jnp.float32)
        o_copy.wait()
        total = None
        for copy, (s, n) in zip(g_copies, g_cuts):
            copy.wait()
            term = lax.dot_general(o_v[:, s : s + n], g_v[:, s : s + n], NT, preferred_element_type=jnp.float32)
            total = term if total is None else total + term
        out_ref[rin : rin + rout, :] = total
        e_copy.wait()

    hbm = pl.BlockSpec(memory_space=pltpu.HBM)
    vmem = pl.BlockSpec(memory_space=pltpu.VMEM)
    operands = (acts, out_grads, in_t, out_t, example_ids, query_ids)
    return pl.pallas_call(
        kernel,
        out_shape=[
            jax.ShapeDtypeStruct((rin + rout, tok), jnp.float32),
            jax.ShapeDtypeStruct(example_ids.shape, example_ids.dtype),
            jax.ShapeDtypeStruct((count * E_DEV, queries), jnp.bfloat16),
        ],
        in_specs=[hbm] * 6,
        out_specs=[vmem] * 3,
        scratch_shapes=[
            pltpu.VMEM(acts.shape, acts.dtype),
            pltpu.VMEM(out_grads.shape, out_grads.dtype),
            pltpu.VMEM(in_t.shape, in_t.dtype),
            pltpu.VMEM(out_t.shape, out_t.dtype),
            pltpu.VMEM(query_ids.shape, query_ids.dtype),
            pltpu.SemaphoreType.DMA((5 + len(g_cuts),)),
        ],
        compiler_params=pltpu.CompilerParams(vmem_limit_bytes=16 * 2**20),
        name="project",
    )(*[pltpu.with_memory_space_constraint(x, pltpu.HBM) for x in operands])


def sketch(mine, other, ids, rin):
    rout = mine.shape[0] - rin
    tok = mine.shape[1]
    groups = LANES // rin
    o_per = rout // groups

    def kernel(mine_ref, other_ref, ids_ref, out_ref):
        both = (mine_ref[...] + other_ref[...]).astype(jnp.bfloat16)
        left = both[0:rin]
        right = both[rin : rin + rout].astype(jnp.float32)
        member = lax.broadcasted_iota(jnp.int32, (E_DEV, tok), 0) == ids_ref[...]
        member = jnp.where(member, 1.0, 0.0)
        zero = jnp.zeros((rin, tok), jnp.bfloat16)
        columns, rows = [], []
        for g in range(groups):
            masked = [member * right[g * o_per + o : g * o_per + o + 1] for o in range(o_per)]
            columns.append(jnp.concatenate(masked, axis=0).astype(jnp.bfloat16))
            rows.append(jnp.concatenate([left if h == g else zero for h in range(groups)], axis=1))
        out_ref[...] = lax.dot_general(
            jnp.concatenate(columns, axis=1),
            jnp.concatenate(rows, axis=0),
            NT,
            preferred_element_type=jnp.float32,
        ).astype(jnp.bfloat16)

    return pl.pallas_call(
        kernel,
        out_shape=jax.ShapeDtypeStruct((o_per * E_DEV, LANES), jnp.bfloat16),
        compiler_params=pltpu.CompilerParams(vmem_limit_bytes=4 * 2**20),
        name="sketch",
    )(mine, other, ids)


def solve(blocks, pick):
    count = len(blocks)
    size = count * E_DEV
    k_size = blocks[0].shape[0] * LANES // E_DEV
    queries = pick.shape[1]
    group = 2
    span = group * E_DEV

    def kernel(*refs):
        block_refs, pick_ref, out_ref, basis = refs[:count], refs[count], refs[count + 1], refs[count + 2]

        def flat(ref):
            block = ref[...].astype(jnp.float32)
            cuts = [block[r : r + E_DEV] for r in range(0, block.shape[0], E_DEV)]
            return jnp.concatenate(cuts, axis=1)

        flats = [flat(ref) for ref in block_refs]
        every = jnp.concatenate(flats, axis=0).astype(jnp.bfloat16)
        twice = jnp.concatenate([every, every], axis=0)
        gram = lax.dot_general(every, twice, NT, preferred_element_type=jnp.float32)
        squares = sum(f * f for f in flats)
        squares = sum(squares[:, s : s + LANES] for s in range(0, k_size, LANES))
        total = jnp.sum(jnp.sum(squares, axis=0, keepdims=True), axis=1, keepdims=True)
        shape = (E_DEV, 2 * size)
        damping = jnp.broadcast_to(total * (0.1 / k_size), shape)
        row = lax.broadcasted_iota(jnp.int32, gram.shape, 0)
        lane = lax.broadcasted_iota(jnp.int32, gram.shape, 1)
        diagonal = row == lane
        system = jnp.where(lane < size, jnp.where(diagonal, 1.0, 0.0), gram)
        table = [system[r : r + E_DEV] for r in range(0, size, E_DEV)]
        sub = lax.broadcasted_iota(jnp.int32, shape, 0)
        lane = lax.broadcasted_iota(jnp.int32, shape, 1)
        here = [sub == i for i in range(E_DEV)]
        norms = jnp.sum(jnp.where(diagonal, gram, 0.0), axis=1, keepdims=True)
        norms = [jnp.broadcast_to(norms[r : r + E_DEV], shape) for r in range(0, size, E_DEV)]
        spread = jnp.zeros(shape, jnp.float32)

        def down(value, i):
            return jnp.broadcast_to(value[i : i + 1], shape)

        left = set(range(count))
        for first in [*range(group, count, group), 0]:
            own = range(group)
            base = size + first * E_DEV
            wide = {
                r: [jnp.broadcast_to(table[r][:, c : c + 1], shape) for c in range(base, base + span)] for r in sorted(left)
            }
            left -= {first + k for k in own}
            rows = [table[first + k] + jnp.where(lane == sub + (base + k * E_DEV), damping, 0.0) for k in own]
            cols = [list(wide[first + k]) for k in own]
            for j in range(span):
                k = j // E_DEV
                cols[k][j] = cols[k][j] + jnp.where(here[j % E_DEV], damping, 0.0)
            scalings = []
            for i in range(0, span, 2):
                which, at = i // E_DEV, i % E_DEV
                p, q = down(cols[which][i], at), down(cols[which][i + 1], at)
                s, t = down(cols[which][i], at + 1), down(cols[which][i + 1], at + 1)
                inverse = 1.0 / (p * t - q * s)
                scalings.append((t * inverse, q * inverse, p * inverse, s * inverse))
                norm = norms[first + which]
                spread = spread + jnp.abs(down(norm, at) * scalings[-1][0]) + jnp.abs(down(norm, at + 1) * scalings[-1][2])
                factors = []
                for k in own:
                    x, y = cols[k][i], cols[k][i + 1]
                    pair = (x * t - y * s, y * p - x * q)
                    if k == which:
                        pair = [jnp.where(here[at] | here[at + 1], 0.0, f) for f in pair]
                    factors.append([f * inverse for f in pair])

                def clear(values):
                    upper, lower = down(values[which], at), down(values[which], at + 1)
                    return [values[k] - (factors[k][0] * upper + factors[k][1] * lower) for k in own]

                for j in range(i + 2, span):
                    fresh = clear([cols[k][j] for k in own])
                    for k in own:
                        cols[k][j] = fresh[k]
                rows = clear(rows)
            for k in own:
                scaled = rows[k]
                for at in range(0, E_DEV, 2):
                    a, b, c, d = scalings[(k * E_DEV + at) // 2]
                    upper, lower = down(rows[k], at), down(rows[k], at + 1)
                    scaled = jnp.where(here[at], a * upper - b * lower, scaled)
                    scaled = jnp.where(here[at + 1], c * lower - d * upper, scaled)
                table[first + k] = scaled
            lines = [down(table[first + j // E_DEV], j % E_DEV) for j in range(span)]
            for r in sorted(left):
                terms = [wide[r][j] * lines[j] for j in range(span)]
                while len(terms) > 1:
                    terms = [x + y for x, y in zip(terms[::2], terms[1::2])]
                table[r] = table[r] - terms[0]

        eye = jnp.where(sub == lane, 1.0, 0.0)

        def picked(result):
            result = result[:, 0:size]
            high = result.astype(jnp.bfloat16).astype(jnp.float32)
            mid = (result - high).astype(jnp.bfloat16).astype(jnp.float32)
            parts = jnp.concatenate([high, mid, result - high - mid], axis=0).astype(jnp.bfloat16)
            found = jnp.dot(parts, pick_ref[...], preferred_element_type=jnp.float32)
            return found[0:E_DEV] + (found[E_DEV : 2 * E_DEV] + found[2 * E_DEV : 3 * E_DEV])

        out_ref[...] = picked(eye - damping * table[0])

        @pl.when(jnp.logical_not(spread[0, 0] <= 4.0 * size))
        def _():
            for k, ref in enumerate(block_refs):
                basis[k * E_DEV : (k + 1) * E_DEV, 0:k_size] = flat(ref)
            root = jnp.sqrt(damping[0:1, :])
            basis[:, k_size : k_size + 2 * size] = jnp.where(diagonal, jnp.broadcast_to(root, gram.shape), 0.0)
            number = lax.broadcasted_iota(jnp.int32, (size, 1), 0)

            def step(i, carry):
                line = basis[pl.ds(i, 1), :]
                line = line / jnp.sqrt(jnp.sum(line * line, axis=1, keepdims=True))
                everything = basis[...]
                part = jnp.sum(everything * line, axis=1, keepdims=True)
                part = jnp.where(number > i, part, 0.0)
                basis[...] = jnp.where(number == i, line, everything - part * line)
                return carry

            lax.fori_loop(0, size, step, 0)
            tail = basis[:, k_size : k_size + 2 * size]
            rest = lax.dot_general(
                tail, tail, (((0,), (0,)), ((), ())), precision=lax.Precision.HIGHEST, preferred_element_type=jnp.float32
            )
            out_ref[...] = picked(eye - rest[0:E_DEV])

    vmem = pl.BlockSpec(memory_space=pltpu.VMEM)
    return pl.pallas_call(
        kernel,
        out_shape=jax.ShapeDtypeStruct((E_DEV, queries), jnp.float32),
        in_specs=[vmem] * (count + 1),
        out_specs=vmem,
        scratch_shapes=[pltpu.VMEM((size, k_size + 2 * size), jnp.float32)],
        compiler_params=pltpu.CompilerParams(vmem_limit_bytes=8 * 2**20),
        name="solve",
    )(*blocks, pick)


def fetch(value, step):
    return lax.ppermute(value, ("dp", "mp"), list(enumerate(step)))


def swap(value):
    return lax.ppermute(value, "mp", [(0, 1), (1, 0)])


def local_small(acts, out_grads, in_proj, out_proj, example_ids, query_ids):
    count = lax.axis_size("dp")
    mine, ids, pick = project(
        acts, out_grads, in_proj.T, out_proj.T, example_ids, query_ids.reshape(1, -1), count
    )
    own = sketch(mine, swap(mine), ids, in_proj.shape[1])
    near = [fetch(own, step) for step in STEPS]
    far = [swap(block) for block in near[1:]]
    return solve([own] + near + far, pick).T


def chol_solve(factor, rhs):
    inner = lax.linalg.triangular_solve(factor, rhs, left_side=True, lower=True)
    return lax.linalg.triangular_solve(factor, inner, left_side=True, lower=True, transpose_a=True)


def local_large(acts, out_grads, in_proj, out_proj, example_ids, query_ids):
    part_in = jnp.dot(acts, in_proj, preferred_element_type=jnp.float32)
    part_out = jnp.dot(out_grads, out_proj, preferred_element_type=jnp.float32)
    full_in, full_out = lax.psum((part_in, part_out), "mp")
    left = full_in.astype(jnp.bfloat16)
    right = full_out.astype(jnp.bfloat16)
    tok_count = left.shape[0]
    rin_size = left.shape[1]
    rout_size = right.shape[1]
    k_size = rin_size * rout_size
    ids = example_ids[0]
    onehot = (ids[:, None] == jnp.arange(E_DEV, dtype=jnp.int32)[None, :]).astype(jnp.bfloat16)
    wide = (onehot[:, :, None] * left[:, None, :]).reshape(tok_count, E_DEV * rin_size)
    summed = lax.dot_general(
        right, wide, (((0,), (0,)), ((), ())), preferred_element_type=jnp.float32
    )
    local_sk = (
        summed.reshape(rout_size, E_DEV, rin_size)
        .transpose(1, 0, 2)
        .reshape(E_DEV, k_size)
        .astype(jnp.bfloat16)
    )
    every_sk = lax.all_gather(local_sk, "dp", axis=0, tiled=True)
    gram = lax.dot_general(
        every_sk, every_sk, (((0,), (0,)), ((), ())), preferred_element_type=jnp.float32
    )
    local_f32 = local_sk.astype(jnp.float32)
    total_sq = lax.psum(jnp.sum(local_f32 * local_f32), "dp")
    damping = 0.1 * total_sq / k_size
    damped = gram + damping * jnp.eye(k_size, dtype=jnp.float32)
    factor = jnp.linalg.cholesky(damped)
    queried = jnp.take(every_sk, query_ids, axis=0).astype(jnp.float32)
    precond = chol_solve(factor, queried.T)
    return lax.dot_general(
        precond, local_f32, (((0,), (1,)), ((), ())), precision=lax.Precision.HIGHEST
    )


def solution(mesh):
    in_specs = (
        P(("groups", "dp"), "mp"),
        P(("groups", "dp"), "mp"),
        P("mp", None),
        P("mp", None),
        P(("groups", "dp"), None),
        P(("groups", "mp")),
    )
    out_specs = P(("groups", "mp"), "dp")
    small = mesh.shape["dp"] == 8 and mesh.shape["mp"] == 2
    local = local_small if small else local_large
    return jax.shard_map(local, mesh=mesh, in_specs=in_specs, out_specs=out_specs, check_vma=False)
```

```python
import jax
import jax.numpy as jnp
from jax import lax
from jax.experimental import pallas as pl
from jax.experimental.pallas import tpu as pltpu
from jax.sharding import PartitionSpec as P

E_DEV = 8
LANES = 128
NT = (((1,), (1,)), ((), ()))
STEPS = (
    (9, 8, 13, 12, 1, 0, 15, 14, 6, 7, 5, 4, 11, 10, 3, 2),
    (13, 14, 7, 0, 10, 3, 8, 2, 5, 1, 6, 12, 4, 15, 9, 11),
    (11, 5, 10, 9, 13, 15, 12, 0, 2, 14, 8, 3, 6, 1, 7, 4),
    (7, 3, 4, 14, 8, 6, 10, 5, 12, 11, 15, 0, 2, 9, 13, 1),
)


def places(device):
    blocks = [device // 2]
    blocks += [step.index(device) // 2 for step in STEPS]
    blocks += [step.index(device ^ 1) // 2 for step in STEPS[1:]]
    return sum(blocks.index(owner) << (4 * owner) for owner in range(len(blocks)))


def chunks(size, parts):
    per = -(-size // (parts * LANES)) * LANES
    starts = range(0, size, per)
    return [(s, min(per, size - s)) for s in starts]


def project(acts, out_grads, in_t, out_t, example_ids, query_ids, count):
    rin, rout = in_t.shape[0], out_t.shape[0]
    tok = acts.shape[0]
    queries = query_ids.shape[1]
    g_cuts = chunks(out_grads.shape[1], 2)

    def kernel(a_hbm, g_hbm, i_hbm, o_hbm, e_hbm, q_hbm, out_ref, e_ref, pick_ref, a_v, g_v, i_v, o_v, q_v, sems):
        copies = []

        def start(src, dst):
            copy = pltpu.make_async_copy(src, dst, sems.at[len(copies)])
            copy.start()
            copies.append(copy)
            return copy

        q_copy = start(q_hbm, q_v)
        i_copy = start(i_hbm, i_v)
        a_copy = start(a_hbm, a_v)
        o_copy = start(o_hbm, o_v)
        g_copies = [start(g_hbm.at[:, pl.ds(s, n)], g_v.at[:, pl.ds(s, n)]) for s, n in g_cuts]
        e_copy = start(e_hbm, e_ref)
        q_copy.wait()
        device = lax.axis_index("dp") * 2 + lax.axis_index("mp")
        code = jnp.int32(0)
        for n in range(2 * count):
            bits = places(n)
            code = jnp.where(device == n, bits - (bits >> 31 << 32), code)
        ids = q_v[...]
        spot = ((code >> (ids // E_DEV * 4)) & 7) * E_DEV + ids % E_DEV
        row = lax.broadcasted_iota(jnp.int32, pick_ref.shape, 0)
        pick_ref[...] = jnp.where(row == spot, 1.0, 0.0).astype(jnp.bfloat16)
        i_copy.wait()
        a_copy.wait()
        out_ref[0:rin, :] = lax.dot_general(i_v[...], a_v[...], NT, preferred_element_type=jnp.float32)
        o_copy.wait()
        total = None
        for copy, (s, n) in zip(g_copies, g_cuts):
            copy.wait()
            term = lax.dot_general(o_v[:, s : s + n], g_v[:, s : s + n], NT, preferred_element_type=jnp.float32)
            total = term if total is None else total + term
        out_ref[rin : rin + rout, :] = total
        e_copy.wait()

    hbm = pl.BlockSpec(memory_space=pltpu.HBM)
    vmem = pl.BlockSpec(memory_space=pltpu.VMEM)
    operands = (acts, out_grads, in_t, out_t, example_ids, query_ids)
    return pl.pallas_call(
        kernel,
        out_shape=[
            jax.ShapeDtypeStruct((rin + rout, tok), jnp.float32),
            jax.ShapeDtypeStruct(example_ids.shape, example_ids.dtype),
            jax.ShapeDtypeStruct((count * E_DEV, queries), jnp.bfloat16),
        ],
        in_specs=[hbm] * 6,
        out_specs=[vmem] * 3,
        scratch_shapes=[
            pltpu.VMEM(acts.shape, acts.dtype),
            pltpu.VMEM(out_grads.shape, out_grads.dtype),
            pltpu.VMEM(in_t.shape, in_t.dtype),
            pltpu.VMEM(out_t.shape, out_t.dtype),
            pltpu.VMEM(query_ids.shape, query_ids.dtype),
            pltpu.SemaphoreType.DMA((5 + len(g_cuts),)),
        ],
        compiler_params=pltpu.CompilerParams(vmem_limit_bytes=16 * 2**20),
        name="project",
    )(*[pltpu.with_memory_space_constraint(x, pltpu.HBM) for x in operands])


def sketch(mine, other, ids, rin):
    rout = mine.shape[0] - rin
    tok = mine.shape[1]
    groups = LANES // rin
    o_per = rout // groups

    def kernel(mine_ref, other_ref, ids_ref, out_ref):
        both = (mine_ref[...] + other_ref[...]).astype(jnp.bfloat16)
        left = both[0:rin]
        right = both[rin : rin + rout].astype(jnp.float32)
        member = lax.broadcasted_iota(jnp.int32, (E_DEV, tok), 0) == ids_ref[...]
        member = jnp.where(member, 1.0, 0.0)
        zero = jnp.zeros((rin, tok), jnp.bfloat16)
        columns, rows = [], []
        for g in range(groups):
            masked = [member * right[g * o_per + o : g * o_per + o + 1] for o in range(o_per)]
            columns.append(jnp.concatenate(masked, axis=0).astype(jnp.bfloat16))
            rows.append(jnp.concatenate([left if h == g else zero for h in range(groups)], axis=1))
        out_ref[...] = lax.dot_general(
            jnp.concatenate(columns, axis=1),
            jnp.concatenate(rows, axis=0),
            NT,
            preferred_element_type=jnp.float32,
        ).astype(jnp.bfloat16)

    return pl.pallas_call(
        kernel,
        out_shape=jax.ShapeDtypeStruct((o_per * E_DEV, LANES), jnp.bfloat16),
        compiler_params=pltpu.CompilerParams(vmem_limit_bytes=4 * 2**20),
        name="sketch",
    )(mine, other, ids)


def solve(blocks, pick):
    count = len(blocks)
    size = count * E_DEV
    k_size = blocks[0].shape[0] * LANES // E_DEV
    queries = pick.shape[1]
    group = 2
    span = group * E_DEV

    def kernel(*refs):
        block_refs, pick_ref, out_ref, basis = refs[:count], refs[count], refs[count + 1], refs[count + 2]

        def flat(ref):
            block = ref[...].astype(jnp.float32)
            cuts = [block[r : r + E_DEV] for r in range(0, block.shape[0], E_DEV)]
            return jnp.concatenate(cuts, axis=1)

        flats = [flat(ref) for ref in block_refs]
        every = jnp.concatenate(flats, axis=0).astype(jnp.bfloat16)
        twice = jnp.concatenate([every, every], axis=0)
        gram = lax.dot_general(every, twice, NT, preferred_element_type=jnp.float32)
        squares = sum(f * f for f in flats)
        squares = sum(squares[:, s : s + LANES] for s in range(0, k_size, LANES))
        total = jnp.sum(jnp.sum(squares, axis=0, keepdims=True), axis=1, keepdims=True)
        shape = (E_DEV, 2 * size)
        damping = jnp.broadcast_to(total * (0.1 / k_size), shape)
        row = lax.broadcasted_iota(jnp.int32, gram.shape, 0)
        lane = lax.broadcasted_iota(jnp.int32, gram.shape, 1)
        diagonal = row == lane
        system = jnp.where(lane < size, jnp.where(diagonal, 1.0, 0.0), gram)
        table = [system[r : r + E_DEV] for r in range(0, size, E_DEV)]
        sub = lax.broadcasted_iota(jnp.int32, shape, 0)
        lane = lax.broadcasted_iota(jnp.int32, shape, 1)
        here = [sub == i for i in range(E_DEV)]
        norms = jnp.sum(jnp.where(diagonal, gram, 0.0), axis=1, keepdims=True)
        norms = [jnp.broadcast_to(norms[r : r + E_DEV], shape) for r in range(0, size, E_DEV)]
        spread = jnp.zeros(shape, jnp.float32)

        def down(value, i):
            return jnp.broadcast_to(value[i : i + 1], shape)

        left = set(range(count))
        for first in [*range(group, count, group), 0]:
            own = range(group)
            base = size + first * E_DEV
            wide = {
                r: [jnp.broadcast_to(table[r][:, c : c + 1], shape) for c in range(base, base + span)] for r in sorted(left)
            }
            left -= {first + k for k in own}
            rows = [table[first + k] + jnp.where(lane == sub + (base + k * E_DEV), damping, 0.0) for k in own]
            cols = [list(wide[first + k]) for k in own]
            for j in range(span):
                k = j // E_DEV
                cols[k][j] = cols[k][j] + jnp.where(here[j % E_DEV], damping, 0.0)
            scalings = []
            for i in range(0, span, 2):
                which, at = i // E_DEV, i % E_DEV
                p, q = down(cols[which][i], at), down(cols[which][i + 1], at)
                s, t = q, down(cols[which][i + 1], at + 1)
                inverse = 1.0 / (p * t - q * s)
                scalings.append((t * inverse, q * inverse, p * inverse, s * inverse))
                norm = norms[first + which]
                spread = spread + jnp.abs(down(norm, at) * scalings[-1][0]) + jnp.abs(down(norm, at + 1) * scalings[-1][2])
                factors = []
                for k in own:
                    x, y = cols[k][i], cols[k][i + 1]
                    pair = (x * t - y * s, y * p - x * q)
                    if k == which:
                        pair = [jnp.where(here[at] | here[at + 1], 0.0, f) for f in pair]
                    factors.append([f * inverse for f in pair])

                def clear(values):
                    upper, lower = down(values[which], at), down(values[which], at + 1)
                    return [values[k] - (factors[k][0] * upper + factors[k][1] * lower) for k in own]

                for j in range(i + 2, span):
                    fresh = clear([cols[k][j] for k in own])
                    for k in own:
                        cols[k][j] = fresh[k]
                rows = clear(rows)
            for k in own:
                scaled = rows[k]
                for at in range(0, E_DEV, 2):
                    a, b, c, d = scalings[(k * E_DEV + at) // 2]
                    upper, lower = down(rows[k], at), down(rows[k], at + 1)
                    scaled = jnp.where(here[at], a * upper - b * lower, scaled)
                    scaled = jnp.where(here[at + 1], c * lower - d * upper, scaled)
                table[first + k] = scaled
            lines = [down(table[first + j // E_DEV], j % E_DEV) for j in range(span)]
            for r in sorted(left):
                terms = [wide[r][j] * lines[j] for j in range(span)]
                while len(terms) > 1:
                    terms = [x + y for x, y in zip(terms[::2], terms[1::2])]
                table[r] = table[r] - terms[0]

        eye = jnp.where(sub == lane, 1.0, 0.0)

        def picked(result):
            result = result[:, 0:size]
            high = result.astype(jnp.bfloat16).astype(jnp.float32)
            mid = (result - high).astype(jnp.bfloat16).astype(jnp.float32)
            parts = jnp.concatenate([high, mid, result - high - mid], axis=0).astype(jnp.bfloat16)
            found = jnp.dot(parts, pick_ref[...], preferred_element_type=jnp.float32)
            return found[0:E_DEV] + (found[E_DEV : 2 * E_DEV] + found[2 * E_DEV : 3 * E_DEV])

        out_ref[...] = picked(eye - damping * table[0])

        @pl.when(jnp.logical_not(spread[0, 0] <= 4.0 * size))
        def _():
            for k, ref in enumerate(block_refs):
                basis[k * E_DEV : (k + 1) * E_DEV, 0:k_size] = flat(ref)
            root = jnp.sqrt(damping[0:1, :])
            basis[:, k_size : k_size + 2 * size] = jnp.where(diagonal, jnp.broadcast_to(root, gram.shape), 0.0)
            number = lax.broadcasted_iota(jnp.int32, (size, 1), 0)

            def step(i, carry):
                line = basis[pl.ds(i, 1), :]
                line = line / jnp.sqrt(jnp.sum(line * line, axis=1, keepdims=True))
                everything = basis[...]
                part = jnp.sum(everything * line, axis=1, keepdims=True)
                part = jnp.where(number > i, part, 0.0)
                basis[...] = jnp.where(number == i, line, everything - part * line)
                return carry

            lax.fori_loop(0, size, step, 0)
            tail = basis[:, k_size : k_size + 2 * size]
            rest = lax.dot_general(
                tail, tail, (((0,), (0,)), ((), ())), precision=lax.Precision.HIGHEST, preferred_element_type=jnp.float32
            )
            out_ref[...] = picked(eye - rest[0:E_DEV])

    vmem = pl.BlockSpec(memory_space=pltpu.VMEM)
    return pl.pallas_call(
        kernel,
        out_shape=jax.ShapeDtypeStruct((E_DEV, queries), jnp.float32),
        in_specs=[vmem] * (count + 1),
        out_specs=vmem,
        scratch_shapes=[pltpu.VMEM((size, k_size + 2 * size), jnp.float32)],
        compiler_params=pltpu.CompilerParams(vmem_limit_bytes=8 * 2**20),
        name="solve",
    )(*blocks, pick)


def fetch(value, step):
    return lax.ppermute(value, ("dp", "mp"), list(enumerate(step)))


def swap(value):
    return lax.ppermute(value, "mp", [(0, 1), (1, 0)])


def local_small(acts, out_grads, in_proj, out_proj, example_ids, query_ids):
    count = lax.axis_size("dp")
    mine, ids, pick = project(
        acts, out_grads, in_proj.T, out_proj.T, example_ids, query_ids.reshape(1, -1), count
    )
    own = sketch(mine, swap(mine), ids, in_proj.shape[1])
    near = [fetch(own, step) for step in STEPS]
    far = [swap(block) for block in near[1:]]
    return solve([own] + near + far, pick).T


def chol_solve(factor, rhs):
    inner = lax.linalg.triangular_solve(factor, rhs, left_side=True, lower=True)
    return lax.linalg.triangular_solve(factor, inner, left_side=True, lower=True, transpose_a=True)


def local_large(acts, out_grads, in_proj, out_proj, example_ids, query_ids):
    part_in = jnp.dot(acts, in_proj, preferred_element_type=jnp.float32)
    part_out = jnp.dot(out_grads, out_proj, preferred_element_type=jnp.float32)
    full_in, full_out = lax.psum((part_in, part_out), "mp")
    left = full_in.astype(jnp.bfloat16)
    right = full_out.astype(jnp.bfloat16)
    tok_count = left.shape[0]
    rin_size = left.shape[1]
    rout_size = right.shape[1]
    k_size = rin_size * rout_size
    ids = example_ids[0]
    onehot = (ids[:, None] == jnp.arange(E_DEV, dtype=jnp.int32)[None, :]).astype(jnp.bfloat16)
    wide = (onehot[:, :, None] * left[:, None, :]).reshape(tok_count, E_DEV * rin_size)
    summed = lax.dot_general(
        right, wide, (((0,), (0,)), ((), ())), preferred_element_type=jnp.float32
    )
    local_sk = (
        summed.reshape(rout_size, E_DEV, rin_size)
        .transpose(1, 0, 2)
        .reshape(E_DEV, k_size)
        .astype(jnp.bfloat16)
    )
    every_sk = lax.all_gather(local_sk, "dp", axis=0, tiled=True)
    gram = lax.dot_general(
        every_sk, every_sk, (((0,), (0,)), ((), ())), preferred_element_type=jnp.float32
    )
    local_f32 = local_sk.astype(jnp.float32)
    total_sq = lax.psum(jnp.sum(local_f32 * local_f32), "dp")
    damping = 0.1 * total_sq / k_size
    damped = gram + damping * jnp.eye(k_size, dtype=jnp.float32)
    factor = jnp.linalg.cholesky(damped)
    queried = jnp.take(every_sk, query_ids, axis=0).astype(jnp.float32)
    precond = chol_solve(factor, queried.T)
    return lax.dot_general(
        precond, local_f32, (((0,), (1,)), ((), ())), precision=lax.Precision.HIGHEST
    )


def solution(mesh):
    in_specs = (
        P(("groups", "dp"), "mp"),
        P(("groups", "dp"), "mp"),
        P("mp", None),
        P("mp", None),
        P(("groups", "dp"), None),
        P(("groups", "mp")),
    )
    out_specs = P(("groups", "mp"), "dp")
    small = mesh.shape["dp"] == 8 and mesh.shape["mp"] == 2
    local = local_small if small else local_large
    return jax.shard_map(local, mesh=mesh, in_specs=in_specs, out_specs=out_specs, check_vma=False)
```
